1024 devices in a mesh: gx: 32 (over z), gy: 8 (over y, core), gz: 4 (over x).
Axes of the slice: x: 4, y: 4, z: 32, core: 2. Of those that a mesh axis runs over, the one named last changes fastest.
Arguments:
- stiff_blocks: bfloat16 [128, 16, 4, 4, 192, 192], P('gx', 'gy', 'gz'), may hold values from -6 to 6
- stiff_cols: int32 [128, 16, 4, 4], P('gx', 'gy', 'gz'), may hold values from 0 to 8191, as said below
- prolong_blocks: bfloat16 [128, 16, 4, 4, 6, 192], P('gx', 'gy', 'gz'), may hold values from -0.4375 to 0.4375
- prolong_cols: int32 [128, 16, 4, 4], P('gx', 'gy', 'gz'), may hold values from 0 to 8191, as said below
- agg_nodes: int32 [128, 16, 4], P('gx', 'gy', 'gz'), may hold values from 32 to 64
- row_owner: int32 [32, 8, 4, 8, 1], P('gx', None, 'gz'), may hold values from 0 to 7; in each aligned block of 8 rows (0 to 7, 8 to 15, ..., all dimensions but the last counted through in order) at most 2 rows name the same one
Outputs:
- coarse_owned: float32 [32, 64, 4, 2, 2268], P('gx', 'gy', 'gz')
The draws below stay inside these ranges and needn't reach their ends.
Inputs may be any that keep to these rules, and one draw needn't show every extreme that they name: `stiff_cols`: entry 0 is the aggregate's own id; the other 3 are distinct aggregates sharing a face with it. `prolong_cols`: entry 0 is the aggregate's own id; the other 3 are distinct aggregates sharing a face with it. `row_owner`: within the 8 rows of one block no rank is named more than 2 times, and in some blocks one rank is named exactly 2 times.
All inputs are finite; a program needn't handle non-finite values.
Results may differ from the reference program's by a relative error of at most 0.0029.
Values may be sent and summed in bfloat16 or wider, within the bound.
A program may use at most 32 MiB of HBM per device.

```python
import math
import jax
import jax.numpy as jnp
import numpy as np
from jax import lax

NODES = 64
ROWS = 192
MODES = 6
KA = 4
KP = 4
BALL = 63
AX = 4
AY = 2
AZ = 1
NA = 8
GX = 128
GY = 16
GZ = 4
CAP = 2
N_GX = 32
N_GY = 8
N_GZ = 4


def face_pick(key, slot_count):
    grid_shape = (GX, GY, GZ)
    coord_x = lax.broadcasted_iota(jnp.int32, grid_shape, 0)
    coord_y = lax.broadcasted_iota(jnp.int32, grid_shape, 1)
    coord_z = lax.broadcasted_iota(jnp.int32, grid_shape, 2)
    steps_x = jnp.array([1, -1, 0, 0, 0, 0], jnp.int32)
    steps_y = jnp.array([0, 0, 1, -1, 0, 0], jnp.int32)
    steps_z = jnp.array([0, 0, 0, 0, 1, -1], jnp.int32)
    near_x = coord_x[..., None] + steps_x
    near_y = coord_y[..., None] + steps_y
    near_z = coord_z[..., None] + steps_z
    inside = (near_x >= 0) & (near_x < GX) & (near_y >= 0) & (near_y < GY) & (near_z >= 0) & (near_z < GZ)
    scores = jax.random.randint(key, grid_shape + (6,), 0, 1 << 20) * 8 + jnp.arange(6, dtype=jnp.int32)
    scores = jnp.where(inside, scores, 1 << 28)
    ranking = jnp.argsort(scores, axis=-1)[..., :slot_count - 1]
    pick_x = jnp.take_along_axis(near_x, ranking, axis=-1)
    pick_y = jnp.take_along_axis(near_y, ranking, axis=-1)
    pick_z = jnp.take_along_axis(near_z, ranking, axis=-1)
    own_id = (coord_x * GY + coord_y) * GZ + coord_z
    near_ids = (pick_x * GY + pick_y) * GZ + pick_z
    return jnp.concatenate([own_id[..., None], near_ids], axis=-1).astype(jnp.int32)


def draw_stiff_cols(key, part):
    key = jax.random.fold_in(key, 11)
    return face_pick(key, KA)


def draw_prolong_cols(key, part):
    key = jax.random.fold_in(key, 23)
    return face_pick(key, KP)


def place_ends(values, own_key, least, largest):
    longest = values.shape.index(max(values.shape))
    spots = []
    for shift in (0, 1):
        where = [jax.random.randint(jax.random.fold_in(own_key, axis), (), 0, length) for axis, length in enumerate(values.shape)]
        where[longest] = (where[longest] + shift) % values.shape[longest]
        spots.append(tuple(where))
    return values.at[spots[0]].set(least).at[spots[1]].set(largest)


def steps_of(key, dims, shards, smallest, top_value):
    gain = 1.0
    for axis_at, shards_of in shards:
        steps = jax.random.uniform(jax.random.fold_in(jax.random.fold_in(key, 6), axis_at), (shards_of,), jnp.float32, smallest / len(shards), top_value / len(shards))
        gain = gain * jnp.repeat(jnp.exp(steps), dims[axis_at] // shards_of).reshape((-1,) + (1,) * (len(dims) - 1 - axis_at))
    return gain


def deal_out(rng, own, number, rows, count, top, bound, slope):
    sequence = jax.random.permutation(rng, count)
    packed, ordinary = portions_of(count, rows * top, bound, slope, True), portions_of(count, rows * top, bound, slope, False)
    places = jnp.arange(count)

    def named(lengths, turn):
        used = int((lengths > 0).sum())
        fixed = max(1, used // 4)
        passed = fixed + (places - fixed + turn * (used - fixed)) % max(1, count - fixed)
        return jnp.zeros((count,), jnp.int32).at[sequence[jnp.where(places < fixed, places, passed)]].set(jnp.asarray(lengths, jnp.int32))

    lengths = jnp.where(number % 4 == 0, named(packed, number // 4), named(ordinary, number - number // 4 - 1))
    mixed = jax.random.permutation(jax.random.fold_in(own, 3), count)
    giver, receiver = mixed[0:count // 2 * 2:2], mixed[1:count // 2 * 2:2]
    margin = jnp.minimum(lengths[giver] - 1, bound - lengths[receiver]) // 2
    margin = jnp.where((giver == sequence[0]) | (receiver == sequence[0]) | (lengths[receiver] == 0), 0, jnp.maximum(margin, 0))
    passed = jax.random.randint(jax.random.fold_in(own, 4), (count // 2,), 0, 1 << 20) % (margin + 1)
    lengths = lengths.at[giver].add(-passed).at[receiver].add(passed)
    items = jnp.searchsorted(jnp.cumsum(lengths), jnp.arange(rows * top), side="right").astype(jnp.int32)
    table = items.reshape(top, rows).T
    table = table[jax.random.permutation(jax.random.fold_in(own, 1), rows)]
    turn = jax.random.randint(jax.random.fold_in(own, 2), (rows, 1), 0, top)
    return jnp.take_along_axis(table, (jnp.arange(top)[None, :] + turn) % top, axis=1)


def portions_of(number_of, total, limit, lean, full):
    portions = [(1 << 20) // math.isqrt(standing ** lean) + 1 for standing in range(1, number_of + 1)]
    largest = limit if full else min(limit, max(-(-total // number_of), total * portions[0] // sum(portions)))
    least = 1 if total - largest >= number_of - 1 else 0
    counts, spare = [largest] + [least] * (number_of - 1), total - largest - least * (number_of - 1)
    while spare > 0:
        candidates = [i for i in range(1, number_of) if counts[i] < largest] or [i for i in range(1, number_of) if counts[i] < limit]
        pool, budget = sum([portions[i] for i in candidates]), spare
        for i in candidates:
            extra = min(limit - counts[i], max(1, budget * portions[i] // pool), spare)
            counts[i] = counts[i] + extra
            spare = spare - extra
    return np.array(counts)


def centred(own_key, dims, deviation, reach, shards=(), kind=jnp.bfloat16):
    values = deviation * jax.random.normal(own_key, dims, jnp.float32)
    if shards:
        values = values * steps_of(own_key, dims, shards, -0.22, 0.18)
    return jnp.clip(values, -reach, reach).astype(kind)


def setup_inputs(seed: int = 0) -> dict:
    keys = jax.random.split(jax.random.key(seed), 7)
    stiff_blocks = centred(keys[0], (GX, GY, GZ, KA, ROWS, ROWS), 1.0, 6.0, ((0, 32), (1, 8), (2, 4)))
    stiff_cols = draw_stiff_cols(jax.random.fold_in(keys[6], 71), 0)
    prolong_blocks = centred(keys[2], (GX, GY, GZ, KP, MODES, ROWS), ROWS ** -0.5, 0.4375, ((0, 32), (1, 8), (2, 4)))
    prolong_cols = draw_prolong_cols(jax.random.fold_in(keys[6], 71), 0)
    agg_nodes = place_ends(jax.random.randint(keys[4], (GX, GY, GZ), NODES // 2, NODES + 1), jax.random.fold_in(keys[4], 1), NODES // 2, NODES).astype(jnp.int32)
    row_owner_keys = jax.random.split(jax.random.fold_in(keys[5], 1), N_GX * N_GY * N_GZ * NA // NA)
    row_owner_turns = jax.random.permutation(jax.random.fold_in(keys[5], 3), N_GX * N_GY * N_GZ * NA // NA)
    row_owner = jax.vmap(lambda own, number: deal_out(jax.random.fold_in(keys[5], 2), own, number, NA, N_GY, 1, CAP, 2))(row_owner_keys, row_owner_turns).reshape((N_GX, N_GY, N_GZ, NA, 1))
    return dict(stiff_blocks=stiff_blocks, stiff_cols=stiff_cols, prolong_blocks=prolong_blocks, prolong_cols=prolong_cols, agg_nodes=agg_nodes, row_owner=row_owner)


def offset_points(radius):
    return [(step_x, step_y, step_z)
            for step_x in range(-radius, radius + 1)
            for step_y in range(-radius, radius + 1)
            for step_z in range(-radius, radius + 1)
            if abs(step_x) + abs(step_y) + abs(step_z) <= radius]


def offset_table(radius):
    return np.array(offset_points(radius), dtype=np.int32)


def box_lookup(radius):
    side_len = 2 * radius + 1
    lookup = [0] * (side_len ** 3)
    for number, triple in enumerate(offset_points(radius)):
        code_at = ((triple[0] + radius) * side_len + triple[1] + radius) * side_len + triple[2] + radius
        lookup[code_at] = number
    return np.array(lookup, dtype=np.int32)


def box_index(offsets, radius):
    side_len = 2 * radius + 1
    shifted = offsets + radius
    return ((shifted[..., 0] * side_len + shifted[..., 1]) * side_len + shifted[..., 2]).astype(jnp.int32)


def decode_ids(agg_ids, whole_y, whole_z):
    return jnp.stack([agg_ids // (whole_y * whole_z), (agg_ids // whole_z) % whole_y, agg_ids % whole_z], axis=-1).astype(jnp.int32)


def reference(stiff_blocks, stiff_cols, prolong_blocks, prolong_cols, agg_nodes, row_owner):
    agg_total = GX * GY * GZ
    plane_count = GY * GZ
    width_out = BALL * MODES * MODES
    live_rows = lax.broadcasted_iota(jnp.int32, (GX, GY, GZ, ROWS), 3) < 3 * agg_nodes[..., None]
    p_live = jnp.where(live_rows[:, :, :, None, None, :], prolong_blocks, jnp.zeros((), prolong_blocks.dtype))
    p_live = p_live.reshape(agg_total, KP, MODES, ROWS)
    stiff_flat = stiff_blocks.reshape(agg_total, KA, ROWS, ROWS)
    positions = decode_ids(jnp.arange(agg_total, dtype=jnp.int32), GY, GZ)
    stiff_ids = stiff_cols.reshape(agg_total, KA)
    prolong_ids = prolong_cols.reshape(agg_total, KP)
    stiff_delta = decode_ids(stiff_ids, GY, GZ) - positions[:, None, :]
    prolong_delta = decode_ids(prolong_ids, GY, GZ) - positions[:, None, :]
    near_lookup = jnp.asarray(box_lookup(2))
    near_pts = jnp.asarray(offset_table(2))
    near_count = near_pts.shape[0]

    def slab_terms(slab):
        start = (slab * plane_count).astype(jnp.int32)
        stiff_part = lax.dynamic_slice_in_dim(stiff_flat, start, plane_count, 0).astype(jnp.float32)
        cols_part = lax.dynamic_slice_in_dim(stiff_ids, start, plane_count, 0)
        delta_part = lax.dynamic_slice_in_dim(stiff_delta, start, plane_count, 0)
        p_near = p_live[cols_part].astype(jnp.float32)
        p_near_delta = prolong_delta[cols_part]
        products = jnp.einsum('nsrm,nstcm->nstcr', stiff_part, p_near)
        near_index = near_lookup[box_index(delta_part[:, :, None, :] + p_near_delta, 2)]
        near_onehot = (near_index[..., None] == jnp.arange(near_count, dtype=jnp.int32)).astype(jnp.float32)
        ap_rows = jnp.einsum('nsto,nstcr->nocr', near_onehot, products, precision=lax.Precision.HIGHEST).astype(jnp.bfloat16)
        p_own = lax.dynamic_slice_in_dim(p_live, start, plane_count, 0).astype(jnp.float32)
        return jnp.einsum('nuar,nocr->nuoac', p_own, ap_rows.astype(jnp.float32))

    coarse_terms = lax.map(slab_terms, jnp.arange(GX, dtype=jnp.int32))
    coarse_terms = coarse_terms.reshape(agg_total * KP * near_count, MODES * MODES)
    ball_lookup = jnp.asarray(box_lookup(3))
    ball_index = ball_lookup[box_index(near_pts[None, None, :, :] - prolong_delta[:, :, None, :], 3)]
    segment_ids = prolong_ids[:, :, None] * BALL + ball_index
    coarse = jax.ops.segment_sum(coarse_terms, segment_ids.reshape(-1), num_segments=agg_total * BALL)
    coarse = coarse.reshape(N_GX, AX, N_GY, AY, N_GZ, AZ, width_out).transpose(0, 2, 4, 1, 3, 5, 6)
    coarse = coarse.reshape(N_GX, N_GY, N_GZ, NA, width_out)
    owners = row_owner[..., 0]
    earlier = lax.broadcasted_iota(jnp.int32, (NA, NA), 1) < lax.broadcasted_iota(jnp.int32, (NA, NA), 0)
    rank_in = jnp.sum(((owners[..., :, None] == owners[..., None, :]) & earlier).astype(jnp.int32), axis=-1)
    selector = ((owners[:, :, :, None, None, :] == jnp.arange(N_GY, dtype=jnp.int32)[:, None, None])
                & (rank_in[:, :, :, None, None, :] == jnp.arange(CAP, dtype=jnp.int32)[:, None])).astype(jnp.float32)
    delivered = jnp.einsum('xyzdcq,xyzql->xdyzcl', selector, coarse, precision=lax.Precision.HIGHEST)
    return delivered.reshape(N_GX, N_GY * N_GY, N_GZ, CAP, width_out)
```

```python
import functools

import jax
import jax.numpy as jnp
import numpy as np
from jax import lax
from jax.experimental import pallas as pl
from jax.experimental.pallas import tpu as pltpu
from jax.sharding import PartitionSpec as P

MESH = pl.DeviceIdType.MESH
F32 = jnp.float32
BF16 = jnp.bfloat16
AX, AY = 4, 2
NA = AX * AY
SLOTS = 4
MODES = 6
ROWS = 192
CAP = 2
WIDTH = 63 * 36
PART = 21 * 36


def points(radius):
    span = range(-radius, radius + 1)
    return [
        (x, y, z) for x in span for y in span for z in span if abs(x) + abs(y) + abs(z) <= radius
    ]


FACES, NEAR, BALL = points(1), points(2), points(3)
SELF = FACES.index((0, 0, 0))


def tables():
    table = np.full((8, 768), -1.0, np.float32)
    for e, step in enumerate(FACES):
        for d, other in enumerate(FACES):
            j = NEAR.index(tuple(p + q for p, q in zip(step, other)))
            for c in range(MODES):
                table[e, j * MODES + c] = d * 8 + c
        for j, near in enumerate(NEAR):
            o = BALL.index(tuple(p - q for p, q in zip(near, step)))
            for c in range(MODES):
                table[e, 256 + (o // 21) * 128 + (o % 21) * MODES + c] = j * MODES + c
    for a in range(MODES):
        for o in range(21):
            for c in range(MODES):
                table[7, o * 36 + a * MODES + c] = a * 128 + o * MODES + c
    return np.repeat(table[:, None], 8, axis=1)


def split(x):
    high = x.astype(BF16)
    return high, (x - high.astype(F32)).astype(BF16)


def dot(a, b):
    return jnp.dot(a, b, preferred_element_type=F32)


def dot_t(a, b):
    return lax.dot_general(a, b, (((1,), (1,)), ((), ())), preferred_element_type=F32)


def halo_place(n, e):
    x, y = n // AY, n % AY
    step = FACES[e]
    if step == (0, 0, 0):
        return n
    if step[0]:
        near = x + step[0]
        if 0 <= near < AX:
            return near * AY + y
        return (8 if step[0] < 0 else 10) + y
    if step[1]:
        near = y + step[1]
        if 0 <= near < AY:
            return x * AY + near
        return (12 if step[1] < 0 else 16) + 2 * (x % 2) + x // 2
    return (20 if step[2] < 0 else 28) + n


def kernel(
    sizes,
    p_ref, scols, pcols, nodes, owners, tables_ref, s_hbm,
    out,
    s_buf, place, order, ps, pm, wb, tbuf, tsx, tsy, tsz, xs, rows, sbuf,
    s_sem, ph_s, ph_r, t_s, t_r, o_s, o_r, own_sem,
):
    n_gx, n_gy, n_gz = sizes
    gx, gy, gz = lax.axis_index("gx"), lax.axis_index("gy"), lax.axis_index("gz")
    whole_y, whole_z = AY * n_gy, n_gz
    axes = (("gx", gx, n_gx), ("gy", gy, n_gy), ("gz", gz, n_gz))

    def beside(d):
        axis, step = next((i, s) for i, s in enumerate(FACES[d]) if s)
        name, at, count = axes[axis]
        return {name: lax.rem(at + step + count, count)}

    barrier = pltpu.get_barrier_semaphore()
    others = [{"gy": lax.rem(gy + r, n_gy)} for r in range(1, n_gy)]
    peers = [beside(d) for d in (0, 6, 2, 4)] + others
    for peer in peers:
        pl.semaphore_signal(barrier, inc=1, device_id=peer, device_id_type=MESH)

    s_copies = []
    for n in range(NA):
        copy = pltpu.make_async_copy(
            s_hbm.at[pl.ds(n * SLOTS, SLOTS)], s_buf.at[pl.ds(n * SLOTS, SLOTS)], s_sem.at[n]
        )
        copy.start()
        s_copies.append(copy)

    def direction(delta):
        found = jnp.int32(SELF)
        for size in (1, whole_z, whole_y * whole_z):
            found = found + (delta >= size).astype(jnp.int32) - (delta <= -size).astype(jnp.int32)
        return found

    p_dir, s_dir = [], []
    for n in range(NA):
        x, y = n // AY, n % AY
        own = ((gx * AX + x) * whole_y + gy * AY + y) * whole_z + gz
        p_dir.append([direction(pcols[x, y, 0, t] - own) for t in range(SLOTS)])
        s_dir.append([direction(scols[x, y, 0, t] - own) for t in range(SLOTS)])

    row32 = lax.broadcasted_iota(jnp.int32, (32, 64), 0)
    lane192 = lax.broadcasted_iota(jnp.int32, (4, ROWS), 1)
    for n in range(NA):
        x, y = n // AY, n % AY
        live = lane192 < 3 * nodes[y, 0, x]
        for c in range(MODES):
            block = p_ref[n, c].astype(F32)
            block = jnp.where(live, block, 0.0)
            ps[0, pl.ds(n * 32 + 4 * c, 4), :] = block[:, :128]
            ps[1, pl.ds(n * 32 + 4 * c, 4), pl.ds(0, 64)] = block[:, 128:]
        ps[0, pl.ds(n * 32 + 24, 8), :] = jnp.zeros((8, 128), F32)
        ps[1, pl.ds(n * 32 + 24, 8), pl.ds(0, 64)] = jnp.zeros((8, 64), F32)
        code = jnp.full((32, 64), p_dir[n][0], jnp.int32)
        for t in range(1, SLOTS):
            code = jnp.where((row32 & 3) == t, p_dir[n][t], code)
        code = jnp.where(row32 < 24, code * 8 + (row32 >> 2), -2)
        ps[1, pl.ds(n * 32, 32), pl.ds(64, 64)] = code.astype(F32)
        for k in range(2):
            pm[x, y, :, pl.ds(k * 128, 128)] = ps[k, pl.ds(n * 32, 32), :].astype(BF16)

    pl.semaphore_wait(barrier, len(peers))

    def halo(i, src, dst, d):
        copy = pltpu.make_async_remote_copy(
            src_ref=src, dst_ref=dst, send_sem=ph_s.at[i], recv_sem=ph_r.at[i],
            device_id=beside(d), device_id_type=MESH,
        )
        copy.start()
        return copy

    halos = [
        halo(0, pm.at[pl.ds(0, 4)], pm.at[pl.ds(14, 4)], 2),
        halo(1, pm.at[pl.ds(0, 4)], pm.at[pl.ds(10, 4)], 4),
        halo(2, pm.at[pl.ds(0, 2), 0], pm.at[pl.ds(8, 2), 0], 1),
        halo(3, pm.at[pl.ds(2, 2), 0], pm.at[pl.ds(8, 2), 1], 1),
        halo(4, pm.at[pl.ds(0, 2), 1], pm.at[pl.ds(6, 2), 0], 5),
        halo(5, pm.at[pl.ds(2, 2), 1], pm.at[pl.ds(6, 2), 1], 5),
        halo(6, pm.at[0], pm.at[5], 0),
        halo(7, pm.at[3], pm.at[4], 6),
    ]

    def one_hot(source, count):
        wide = source.shape[1]
        at = lax.broadcasted_iota(jnp.int32, (count, wide), 0).astype(F32)
        return jnp.where(at == jnp.concatenate([source] * (count // 8), axis=0), 1.0, 0.0).astype(BF16)

    for d in range(7):
        place[d] = one_hot(tables_ref[d, :, pl.ds(256, 384)], 256)
    order[...] = one_hot(tables_ref[7], MODES * 128)

    for n in range(NA):
        halves = []
        for k in range(2):
            parts = [ps[k, pl.ds(n * 32 + t, 8, stride=4), :] for t in range(SLOTS)]
            dense = []
            for d in range(7):
                total = jnp.zeros((8, 128), F32)
                for t in range(SLOTS):
                    mark = jnp.full((8, 128), p_dir[n][t], jnp.int32) == d
                    total = jnp.where(mark, parts[t], total)
                dense.append(total)
            dense.append(jnp.zeros((8, 128), F32))
            halves.append(jnp.concatenate(dense, axis=0))
        dense = jnp.concatenate([halves[0], halves[1][:, :64]], axis=1).astype(BF16)
        s_copies[n].wait()
        for s in range(SLOTS):
            high, low = split(dot(dense, s_buf[n * SLOTS + s]))
            wb[n, pl.ds(s * 128, 64), :] = high
            wb[n, pl.ds(s * 128 + 64, 64), :] = low

    for copy in halos:
        copy.wait()

    lane128 = lax.broadcasted_iota(jnp.int32, (128, 128), 1) // 32

    def term(i, src, dst, d):
        copy = pltpu.make_async_remote_copy(
            src_ref=src, dst_ref=dst, send_sem=t_s.at[i], recv_sem=t_r.at[i],
            device_id=beside(d), device_id_type=MESH,
        )
        copy.start()
        return copy

    terms = {}
    for n in range(NA):
        x, y = n // AY, n % AY
        tables, picks = [], []
        for s in range(SLOTS):
            e = s_dir[n][s]
            at = jnp.int32(halo_place(n, 0))
            for other in range(1, 7):
                at = jnp.where(e == other, halo_place(n, other), at)
            table = pm[at // AY, at % AY]
            tables.append(table[:, :ROWS])
            code = jnp.broadcast_to(table[:, ROWS:ROWS + 1].astype(F32), (32, 256))
            wanted = tables_ref[e, :, pl.ds(0, 256)]
            wanted = jnp.concatenate([wanted] * 4, axis=0)
            picks.append(jnp.where(code == wanted, 1.0, 0.0).astype(BF16))
        full = dot_t(wb[n], jnp.concatenate(tables, axis=0))
        z = jnp.zeros((128, 128), F32)
        for s in range(SLOTS):
            z = jnp.where(lane128 == s, full[s * 128:(s + 1) * 128], z)
        high, low = split(z[:64] + z[64:])
        both = dot(jnp.concatenate([high, low], axis=0), jnp.concatenate(picks, axis=0))
        t_all = both[:64] + both[64:]
        for d, step in enumerate(FACES):
            block = t_all[d * 8:d * 8 + 8]
            to_x, to_y = x + step[0], y + step[1]
            if step[2]:
                tsz[0 if step[2] < 0 else 1, x, y] = block
            elif not 0 <= to_x < AX:
                tsx[0 if step[0] < 0 else 1, y] = block
            elif not 0 <= to_y < AY:
                tsy[0 if step[1] < 0 else 1, x] = block
            else:
                tbuf[d, to_x, to_y] = block
        if n == 1:
            terms[0] = term(0, tsx.at[0], tbuf.at[0, 3], 0)
        if n == NA - 1:
            terms[2] = term(1, tsz.at[0], tbuf.at[2], 2)
            terms[4] = term(2, tsz.at[1], tbuf.at[4], 4)
            terms[1] = term(3, tsy.at[0], tbuf.at[1, :, 1], 1)
            terms[5] = term(4, tsy.at[1], tbuf.at[5, :, 0], 5)
            terms[6] = term(5, tsx.at[1], tbuf.at[6, 0], 6)

    total = jnp.zeros((128, 384), F32)
    for d in (3, 0, 6, 1, 5, 2, 4):
        if d in terms:
            terms[d].wait()
        high, low = split(tbuf[d].reshape(64, 256))
        total = total + dot(jnp.concatenate([high, low], axis=0), place[d])
    total = total[:64] + total[64:]
    for v in range(3):
        xs[v] = total[:, v * 128:v * 128 + 128]

    stacked = []
    for v in range(3):
        stacked.append(
            jnp.concatenate(
                [xs[v, pl.ds(a, 8, stride=8), :] for a in range(MODES)], axis=1
            )
        )
    high, low = split(jnp.concatenate(stacked, axis=0))
    flat = dot(jnp.concatenate([high, low], axis=0), order[...])
    flat = flat[:24] + flat[24:]
    for v in range(3):
        rows[:, pl.ds(v * PART, PART)] = flat[v * 8:v * 8 + 8, :PART]

    owner = [owners[0, gy, 0, 0, q] for q in range(NA)]
    spot = []
    for q in range(NA):
        rank = jnp.int32(0)
        for other in range(q):
            rank = rank + (owner[other] == owner[q]).astype(jnp.int32)
        spot.append(owner[q] * CAP + rank)
    row2 = lax.broadcasted_iota(jnp.int32, (CAP, WIDTH), 0)
    for target in range(n_gy):
        chosen = jnp.zeros((CAP, WIDTH), F32)
        for q in range(NA):
            row = jnp.broadcast_to(rows[pl.ds(q, 1), pl.ds(0, WIDTH)], (CAP, WIDTH))
            chosen = jnp.where(row2 + target * CAP == spot[q], row, chosen)
        sbuf[target] = chosen
    sends = []
    for r in range(1, n_gy):
        target = lax.rem(gy + r, n_gy)
        copy = pltpu.make_async_remote_copy(
            src_ref=sbuf.at[target], dst_ref=out.at[gy], send_sem=o_s.at[r - 1], recv_sem=o_r.at[r - 1],
            device_id={"gy": target}, device_id_type=MESH,
        )
        copy.start()
        sends.append(copy)
    mine = pltpu.make_async_copy(sbuf.at[gy], out.at[gy], own_sem)
    mine.start()
    for copy in sends:
        copy.wait()
    mine.wait()


def local(sizes, stiff_blocks, stiff_cols, prolong_blocks, prolong_cols, agg_nodes, row_owner):
    n_gy = sizes[1]
    smem = pl.BlockSpec(memory_space=pltpu.SMEM)
    vmem = pl.BlockSpec(memory_space=pltpu.VMEM)
    hbm = pl.BlockSpec(memory_space=pltpu.HBM)
    out = pl.pallas_call(
        functools.partial(kernel, sizes),
        out_shape=jax.ShapeDtypeStruct((n_gy, CAP, WIDTH), F32),
        in_specs=[vmem, smem, smem, smem, smem, vmem, hbm],
        out_specs=hbm,
        scratch_shapes=[
            pltpu.VMEM((NA * SLOTS, ROWS, ROWS), BF16),
            pltpu.VMEM((7, 256, 384), BF16),
            pltpu.VMEM((MODES * 128, MODES * 128), BF16),
            pltpu.VMEM((2, NA * 32, 128), F32),
            pltpu.VMEM((18, AY, 32, 256), BF16),
            pltpu.VMEM((NA, 512, ROWS), BF16),
            pltpu.VMEM((7, AX, AY, 8, 256), F32),
            pltpu.VMEM((2, AY, 8, 256), F32),
            pltpu.VMEM((2, AX, 8, 256), F32),
            pltpu.VMEM((2, AX, AY, 8, 256), F32),
            pltpu.VMEM((3, 64, 128), F32),
            pltpu.VMEM((8, 2304), F32),
            pltpu.VMEM((n_gy, CAP, WIDTH), F32),
            pltpu.SemaphoreType.DMA((NA,)),
            pltpu.SemaphoreType.DMA((8,)),
            pltpu.SemaphoreType.DMA((8,)),
            pltpu.SemaphoreType.DMA((6,)),
            pltpu.SemaphoreType.DMA((6,)),
            pltpu.SemaphoreType.DMA((n_gy - 1,)),
            pltpu.SemaphoreType.DMA((n_gy - 1,)),
            pltpu.SemaphoreType.DMA,
        ],
        compiler_params=pltpu.CompilerParams(
            collective_id=0, has_side_effects=True, vmem_limit_bytes=40 * 1024 * 1024
        ),
        name="galerkin",
    )(
        prolong_blocks.transpose(0, 1, 2, 4, 3, 5).reshape(NA, MODES, SLOTS, ROWS),
        stiff_cols,
        prolong_cols,
        agg_nodes.transpose(1, 2, 0),
        row_owner.transpose(0, 1, 2, 4, 3),
        jnp.asarray(tables()),
        stiff_blocks.reshape(NA * SLOTS, ROWS, ROWS),
    )
    return out[None, :, None]


def solution(mesh):
    sizes = (mesh.shape["gx"], mesh.shape["gy"], mesh.shape["gz"])
    return jax.shard_map(
        functools.partial(local, sizes),
        mesh=mesh,
        in_specs=(
            P("gx", "gy", "gz", None, None, None),
            P("gx", "gy", "gz", None),
            P("gx", "gy", "gz", None, None, None),
            P("gx", "gy", "gz", None),
            P("gx", "gy", "gz"),
            P("gx", None, "gz", None, None),
        ),
        out_specs=P("gx", "gy", "gz", None, None),
        check_vma=False,
    )
```

```python
import functools

import jax
import jax.numpy as jnp
import numpy as np
from jax import lax
from jax.experimental import pallas as pl
from jax.experimental.pallas import tpu as pltpu
from jax.sharding import PartitionSpec as P

MESH = pl.DeviceIdType.MESH
F32 = jnp.float32
BF16 = jnp.bfloat16
AX, AY = 4, 2
NA = AX * AY
SLOTS = 4
MODES = 6
ROWS = 192
CAP = 2
WIDTH = 63 * 36
PART = 21 * 36


def points(radius):
    span = range(-radius, radius + 1)
    return [
        (x, y, z) for x in span for y in span for z in span if abs(x) + abs(y) + abs(z) <= radius
    ]


FACES, NEAR, BALL = points(1), points(2), points(3)
SELF = FACES.index((0, 0, 0))


def tables():
    table = np.full((8, 768), -1.0, np.float32)
    for e, step in enumerate(FACES):
        for d, other in enumerate(FACES):
            j = NEAR.index(tuple(p + q for p, q in zip(step, other)))
            for c in range(MODES):
                table[e, j * MODES + c] = d * 8 + c
        for j, near in enumerate(NEAR):
            o = BALL.index(tuple(p - q for p, q in zip(near, step)))
            for c in range(MODES):
                table[e, 256 + (o // 21) * 128 + (o % 21) * MODES + c] = j * MODES + c
    for a in range(MODES):
        for o in range(21):
            for c in range(MODES):
                table[7, o * 36 + a * MODES + c] = a * 128 + o * MODES + c
    return np.repeat(table[:, None], 8, axis=1)


def split(x):
    high = x.astype(BF16)
    return high, (x - high.astype(F32)).astype(BF16)


def dot(a, b):
    return jnp.dot(a, b, preferred_element_type=F32)


def dot_t(a, b):
    return lax.dot_general(a, b, (((1,), (1,)), ((), ())), preferred_element_type=F32)


def halo_place(n, e):
    x, y = n // AY, n % AY
    step = FACES[e]
    if step == (0, 0, 0):
        return n
    if step[0]:
        near = x + step[0]
        if 0 <= near < AX:
            return near * AY + y
        return (8 if step[0] < 0 else 10) + y
    if step[1]:
        near = y + step[1]
        if 0 <= near < AY:
            return x * AY + near
        return (12 if step[1] < 0 else 16) + 2 * (x % 2) + x // 2
    return (20 if step[2] < 0 else 28) + n


def kernel(
    sizes,
    p_hbm, scols_hbm, pcols_hbm, nodes_hbm, owners_hbm, tables_hbm, s_hbm,
    out,
    p_ref, scols, pcols, nodes, owners, tables_ref,
    s_buf, place, order, ps, pm, wb, tbuf, tsx, tsy, tsz, xs, rows, sbuf,
    in_sem, s_sem, ph_s, ph_r, t_s, t_r, o_s, o_r, own_sem,
):
    n_gx, n_gy, n_gz = sizes
    gx, gy, gz = lax.axis_index("gx"), lax.axis_index("gy"), lax.axis_index("gz")
    whole_y, whole_z = AY * n_gy, n_gz
    axes = (("gx", gx, n_gx), ("gy", gy, n_gy), ("gz", gz, n_gz))

    def axis_of(d):
        return next((axes[i] + (step,) for i, step in enumerate(FACES[d]) if step))

    def beside(d):
        name, at, count, step = axis_of(d)
        return {name: at + step}

    def exists(d):
        name, at, count, step = axis_of(d)
        return at > 0 if step < 0 else at < count - 1

    loads = [
        pltpu.make_async_copy(src, dst, in_sem.at[i])
        for i, (src, dst) in enumerate([
            (pcols_hbm, pcols), (nodes_hbm, nodes), (p_hbm, p_ref),
            (scols_hbm, scols), (owners_hbm, owners), (tables_hbm, tables_ref),
        ])
    ]
    for copy in loads:
        copy.start()
    s_copies = []
    for n in range(NA):
        copy = pltpu.make_async_copy(
            s_hbm.at[pl.ds(n * SLOTS, SLOTS)], s_buf.at[pl.ds(n * SLOTS, SLOTS)], s_sem.at[n]
        )
        copy.start()
        s_copies.append(copy)

    barrier = pltpu.get_barrier_semaphore()
    others = [{"gy": lax.rem(gy + r, n_gy)} for r in range(1, n_gy)]
    greeted = jnp.int32(len(others))
    for peer in others:
        pl.semaphore_signal(barrier, inc=1, device_id=peer, device_id_type=MESH)
    for d in (0, 6, 2, 4):
        greeted = greeted + exists(d).astype(jnp.int32)

        @pl.when(exists(d))
        def _():
            pl.semaphore_signal(barrier, inc=1, device_id=beside(d), device_id_type=MESH)

    for copy in loads[:3]:
        copy.wait()

    def direction(delta):
        found = jnp.int32(SELF)
        for size in (1, whole_z, whole_y * whole_z):
            found = found + (delta >= size).astype(jnp.int32) - (delta <= -size).astype(jnp.int32)
        return found

    def own_id(n):
        return ((gx * AX + n // AY) * whole_y + gy * AY + n % AY) * whole_z + gz

    p_dir = []
    for n in range(NA):
        x, y = n // AY, n % AY
        own = own_id(n)
        p_dir.append([direction(pcols[x, y, 0, t] - own) for t in range(SLOTS)])

    row32 = lax.broadcasted_iota(jnp.int32, (32, 64), 0)
    lane192 = lax.broadcasted_iota(jnp.int32, (4, ROWS), 1)
    for n in range(NA):
        x, y = n // AY, n % AY
        live = lane192 < 3 * nodes[y, 0, x]
        for c in range(MODES):
            block = p_ref[n, c].astype(F32)
            block = jnp.where(live, block, 0.0)
            ps[0, pl.ds(n * 32 + 4 * c, 4), :] = block[:, :128]
            ps[1, pl.ds(n * 32 + 4 * c, 4), pl.ds(0, 64)] = block[:, 128:]
        ps[0, pl.ds(n * 32 + 24, 8), :] = jnp.zeros((8, 128), F32)
        ps[1, pl.ds(n * 32 + 24, 8), pl.ds(0, 64)] = jnp.zeros((8, 64), F32)
        code = jnp.full((32, 64), p_dir[n][0], jnp.int32)
        for t in range(1, SLOTS):
            code = jnp.where((row32 & 3) == t, p_dir[n][t], code)
        code = jnp.where(row32 < 24, code * 8 + (row32 >> 2), -2)
        ps[1, pl.ds(n * 32, 32), pl.ds(64, 64)] = code.astype(F32)
        for k in range(2):
            pm[x, y, :, pl.ds(k * 128, 128)] = ps[k, pl.ds(n * 32, 32), :].astype(BF16)

    pl.semaphore_wait(barrier, greeted)

    def exchange(i, src, dst, d, send_sem, recv_sem):
        copy = pltpu.make_async_remote_copy(
            src_ref=src, dst_ref=dst, send_sem=send_sem.at[i], recv_sem=recv_sem.at[i],
            device_id=beside(d), device_id_type=MESH,
        )

        @pl.when(exists(d))
        def _():
            copy.start()

        @pl.when(jnp.logical_not(exists(6 - d)))
        def _():
            dst[...] = jnp.zeros(dst.shape, dst.dtype)

        def arrived():
            @pl.when(exists(6 - d))
            def _():
                copy.wait_recv()

        def sent():
            @pl.when(exists(d))
            def _():
                copy.wait_send()

        return arrived, sent

    def halo(i, src, dst, d):
        return exchange(i, src, dst, d, ph_s, ph_r)

    halos = [
        halo(0, pm.at[pl.ds(0, 4)], pm.at[pl.ds(14, 4)], 2),
        halo(1, pm.at[pl.ds(0, 4)], pm.at[pl.ds(10, 4)], 4),
        halo(2, pm.at[pl.ds(0, 2), 0], pm.at[pl.ds(8, 2), 0], 1),
        halo(3, pm.at[pl.ds(2, 2), 0], pm.at[pl.ds(8, 2), 1], 1),
        halo(4, pm.at[pl.ds(0, 2), 1], pm.at[pl.ds(6, 2), 0], 5),
        halo(5, pm.at[pl.ds(2, 2), 1], pm.at[pl.ds(6, 2), 1], 5),
        halo(6, pm.at[0], pm.at[5], 0),
        halo(7, pm.at[3], pm.at[4], 6),
    ]

    for n in range(NA):
        halves = []
        for k in range(2):
            parts = [ps[k, pl.ds(n * 32 + t, 8, stride=4), :] for t in range(SLOTS)]
            dense = []
            for d in range(7):
                total = jnp.zeros((8, 128), F32)
                for t in range(SLOTS):
                    mark = jnp.full((8, 128), p_dir[n][t], jnp.int32) == d
                    total = jnp.where(mark, parts[t], total)
                dense.append(total)
            dense.append(jnp.zeros((8, 128), F32))
            halves.append(jnp.concatenate(dense, axis=0))
        dense = jnp.concatenate([halves[0], halves[1][:, :64]], axis=1).astype(BF16)
        s_copies[n].wait()
        for s in range(SLOTS):
            high, low = split(dot(dense, s_buf[n * SLOTS + s]))
            wb[n, pl.ds(s * 128, 64), :] = high
            wb[n, pl.ds(s * 128 + 64, 64), :] = low

    for copy in loads[3:]:
        copy.wait()
    s_dir = []
    for n in range(NA):
        x, y = n // AY, n % AY
        s_dir.append([direction(scols[x, y, 0, s] - own_id(n)) for s in range(SLOTS)])
    for arrived, _ in halos:
        arrived()

    lane128 = lax.broadcasted_iota(jnp.int32, (128, 128), 1) // 32

    def term(i, src, dst, d):
        return exchange(i, src, dst, d, t_s, t_r)

    terms = {}
    for n in range(NA):
        x, y = n // AY, n % AY
        tables, picks = [], []
        for s in range(SLOTS):
            e = s_dir[n][s]
            at = jnp.int32(halo_place(n, 0))
            for other in range(1, 7):
                at = jnp.where(e == other, halo_place(n, other), at)
            table = pm[at // AY, at % AY]
            tables.append(table[:, :ROWS])
            code = jnp.broadcast_to(table[:, ROWS:ROWS + 1].astype(F32), (32, 256))
            wanted = tables_ref[e, :, pl.ds(0, 256)]
            wanted = jnp.concatenate([wanted] * 4, axis=0)
            picks.append(jnp.where(code == wanted, 1.0, 0.0).astype(BF16))
        full = dot_t(wb[n], jnp.concatenate(tables, axis=0))
        z = jnp.zeros((128, 128), F32)
        for s in range(SLOTS):
            z = jnp.where(lane128 == s, full[s * 128:(s + 1) * 128], z)
        high, low = split(z[:64] + z[64:])
        both = dot(jnp.concatenate([high, low], axis=0), jnp.concatenate(picks, axis=0))
        t_all = both[:64] + both[64:]
        for d, step in enumerate(FACES):
            block = t_all[d * 8:d * 8 + 8]
            to_x, to_y = x + step[0], y + step[1]
            if step[2]:
                tsz[0 if step[2] < 0 else 1, x, y] = block
            elif not 0 <= to_x < AX:
                tsx[0 if step[0] < 0 else 1, y] = block
            elif not 0 <= to_y < AY:
                tsy[0 if step[1] < 0 else 1, x] = block
            else:
                tbuf[d, to_x, to_y] = block
        if n == 1:
            terms[0] = term(0, tsx.at[0], tbuf.at[0, 3], 0)
        if n == NA - 1:
            terms[2] = term(1, tsz.at[0], tbuf.at[2], 2)
            terms[4] = term(2, tsz.at[1], tbuf.at[4], 4)
            terms[1] = term(3, tsy.at[0], tbuf.at[1, :, 1], 1)
            terms[5] = term(4, tsy.at[1], tbuf.at[5, :, 0], 5)
            terms[6] = term(5, tsx.at[1], tbuf.at[6, 0], 6)

    def one_hot(source, base):
        wide = source.shape[1]
        at = lax.broadcasted_iota(jnp.int32, (128, wide), 0).astype(F32) + base
        return jnp.where(at == jnp.concatenate([source] * 16, axis=0), 1.0, 0.0).astype(BF16)

    for d in (3, 0, 6, 1, 5, 2, 4):
        for k in range(2):
            place[d, pl.ds(k * 128, 128), :] = one_hot(tables_ref[d, :, pl.ds(256, 384)], k * 128.0)
    for a in range(MODES):
        order[pl.ds(a * 128, 128), :] = one_hot(tables_ref[7], a * 128.0)

    total = jnp.zeros((128, 384), F32)
    for d in (3, 0, 6, 1, 5, 2, 4):
        if d in terms:
            terms[d][0]()
        high, low = split(tbuf[d].reshape(64, 256))
        total = total + dot(jnp.concatenate([high, low], axis=0), place[d])
    total = total[:64] + total[64:]
    for v in range(3):
        xs[v] = total[:, v * 128:v * 128 + 128]

    stacked = []
    for v in range(3):
        stacked.append(
            jnp.concatenate(
                [xs[v, pl.ds(a, 8, stride=8), :] for a in range(MODES)], axis=1
            )
        )
    high, low = split(jnp.concatenate(stacked, axis=0))
    flat = dot(jnp.concatenate([high, low], axis=0), order[...])
    flat = flat[:24] + flat[24:]
    for v in range(3):
        rows[:, pl.ds(v * PART, PART)] = flat[v * 8:v * 8 + 8, :PART]

    owner = [owners[0, gy, 0, 0, q] for q in range(NA)]
    spot = []
    for q in range(NA):
        rank = jnp.int32(0)
        for other in range(q):
            rank = rank + (owner[other] == owner[q]).astype(jnp.int32)
        spot.append(owner[q] * CAP + rank)
    row2 = lax.broadcasted_iota(jnp.int32, (CAP, WIDTH), 0)
    for target in range(n_gy):
        chosen = jnp.zeros((CAP, WIDTH), F32)
        for q in range(NA):
            row = jnp.broadcast_to(rows[pl.ds(q, 1), pl.ds(0, WIDTH)], (CAP, WIDTH))
            chosen = jnp.where(row2 + target * CAP == spot[q], row, chosen)
        sbuf[target] = chosen
    sends = []
    for r in range(1, n_gy):
        target = lax.rem(gy + r, n_gy)
        copy = pltpu.make_async_remote_copy(
            src_ref=sbuf.at[target], dst_ref=out.at[gy], send_sem=o_s.at[r - 1], recv_sem=o_r.at[r - 1],
            device_id={"gy": target}, device_id_type=MESH,
        )
        copy.start()
        sends.append(copy)
    mine = pltpu.make_async_copy(sbuf.at[gy], out.at[gy], own_sem)
    mine.start()
    for copy in sends:
        copy.wait()
    mine.wait()
    for _, sent in halos + list(terms.values()):
        sent()


def local(sizes, stiff_blocks, stiff_cols, prolong_blocks, prolong_cols, agg_nodes, row_owner):
    n_gy = sizes[1]
    hbm = pl.BlockSpec(memory_space=pltpu.HBM)
    out = pl.pallas_call(
        functools.partial(kernel, sizes),
        out_shape=jax.ShapeDtypeStruct((n_gy, CAP, WIDTH), F32),
        in_specs=[hbm] * 7,
        out_specs=hbm,
        scratch_shapes=[
            pltpu.VMEM((NA, MODES, SLOTS, ROWS), BF16),
            pltpu.SMEM(stiff_cols.shape, jnp.int32),
            pltpu.SMEM(prolong_cols.shape, jnp.int32),
            pltpu.SMEM((AY, 1, AX), jnp.int32),
            pltpu.SMEM((1, n_gy, 1, 1, NA), jnp.int32),
            pltpu.VMEM((8, 8, 768), F32),
            pltpu.VMEM((NA * SLOTS, ROWS, ROWS), BF16),
            pltpu.VMEM((7, 256, 384), BF16),
            pltpu.VMEM((MODES * 128, MODES * 128), BF16),
            pltpu.VMEM((2, NA * 32, 128), F32),
            pltpu.VMEM((18, AY, 32, 256), BF16),
            pltpu.VMEM((NA, 512, ROWS), BF16),
            pltpu.VMEM((7, AX, AY, 8, 256), F32),
            pltpu.VMEM((2, AY, 8, 256), F32),
            pltpu.VMEM((2, AX, 8, 256), F32),
            pltpu.VMEM((2, AX, AY, 8, 256), F32),
            pltpu.VMEM((3, 64, 128), F32),
            pltpu.VMEM((8, 2304), F32),
            pltpu.VMEM((n_gy, CAP, WIDTH), F32),
            pltpu.SemaphoreType.DMA((6,)),
            pltpu.SemaphoreType.DMA((NA,)),
            pltpu.SemaphoreType.DMA((8,)),
            pltpu.SemaphoreType.DMA((8,)),
            pltpu.SemaphoreType.DMA((6,)),
            pltpu.SemaphoreType.DMA((6,)),
            pltpu.SemaphoreType.DMA((n_gy - 1,)),
            pltpu.SemaphoreType.DMA((n_gy - 1,)),
            pltpu.SemaphoreType.DMA,
        ],
        compiler_params=pltpu.CompilerParams(
            collective_id=0, has_side_effects=True, vmem_limit_bytes=62 * 1024 * 1024
        ),
        name="galerkin",
    )(
        prolong_blocks.transpose(0, 1, 2, 4, 3, 5).reshape(NA, MODES, SLOTS, ROWS),
        stiff_cols,
        prolong_cols,
        agg_nodes.transpose(1, 2, 0),
        row_owner.transpose(0, 1, 2, 4, 3),
        jnp.asarray(tables()),
        stiff_blocks.reshape(NA * SLOTS, ROWS, ROWS),
    )
    return out[None, :, None]


def solution(mesh):
    sizes = (mesh.shape["gx"], mesh.shape["gy"], mesh.shape["gz"])
    return jax.shard_map(
        functools.partial(local, sizes),
        mesh=mesh,
        in_specs=(
            P("gx", "gy", "gz", None, None, None),
            P("gx", "gy", "gz", None),
            P("gx", "gy", "gz", None, None, None),
            P("gx", "gy", "gz", None),
            P("gx", "gy", "gz"),
            P("gx", None, "gz", None, None),
        ),
        out_specs=P("gx", "gy", "gz", None, None),
        check_vma=False,
    )
```

```python
import functools

import jax
import jax.numpy as jnp
import numpy as np
from jax import lax
from jax.experimental import pallas as pl
from jax.experimental.pallas import tpu as pltpu
from jax.sharding import PartitionSpec as P

MESH = pl.DeviceIdType.MESH
F32 = jnp.float32
BF16 = jnp.bfloat16
AX, AY = 4, 2
NA = AX * AY
SLOTS = 4
MODES = 6
ROWS = 192
CAP = 2
WIDTH = 63 * 36
PART = 21 * 36


def points(radius):
    span = range(-radius, radius + 1)
    return [
        (x, y, z) for x in span for y in span for z in span if abs(x) + abs(y) + abs(z) <= radius
    ]


FACES, NEAR, BALL = points(1), points(2), points(3)
SELF = FACES.index((0, 0, 0))


def tables():
    table = np.full((8, 768), -1.0, np.float32)
    for e, step in enumerate(FACES):
        for d, other in enumerate(FACES):
            j = NEAR.index(tuple(p + q for p, q in zip(step, other)))
            for c in range(MODES):
                table[e, j * MODES + c] = d * 8 + c
        for j, near in enumerate(NEAR):
            o = BALL.index(tuple(p - q for p, q in zip(near, step)))
            for c in range(MODES):
                table[e, 256 + (o // 21) * 128 + (o % 21) * MODES + c] = j * MODES + c
    for a in range(MODES):
        for o in range(21):
            for c in range(MODES):
                table[7, o * 36 + a * MODES + c] = a * 128 + o * MODES + c
    return np.repeat(table[:, None], 8, axis=1)


def split(x):
    high = x.astype(BF16)
    return high, (x - high.astype(F32)).astype(BF16)


def dot(a, b):
    return jnp.dot(a, b, preferred_element_type=F32)


def dot_t(a, b):
    return lax.dot_general(a, b, (((1,), (1,)), ((), ())), preferred_element_type=F32)


def halo_place(n, e):
    x, y = n // AY, n % AY
    step = FACES[e]
    if step == (0, 0, 0):
        return n
    if step[0]:
        near = x + step[0]
        if 0 <= near < AX:
            return near * AY + y
        return (4 if step[0] < 0 else 5) * AY + y
    if step[1]:
        near = y + step[1]
        if 0 <= near < AY:
            return x * AY + near
        return (6 + x) * AY + 1 if step[1] < 0 else (10 + x) * AY
    return (14 if step[2] < 0 else 18) * AY + n


def kernel(
    sizes,
    p_hbm, scols_hbm, pcols_hbm, nodes_hbm, owners_hbm, tables_hbm, s_hbm,
    out,
    p_ref, scols, pcols, nodes, owners, tables_ref,
    s_buf, place, order, ps, pm, wb, tbuf, tsx, tsy, tsz, xs, rows, sbuf,
    in_sem, s_sem, ph_s, ph_r, t_s, t_r, o_s, o_r, own_sem,
):
    n_gx, n_gy, n_gz = sizes
    gx, gy, gz = lax.axis_index("gx"), lax.axis_index("gy"), lax.axis_index("gz")
    whole_y, whole_z = AY * n_gy, n_gz
    axes = (("gx", gx, n_gx), ("gy", gy, n_gy), ("gz", gz, n_gz))

    def axis_of(d):
        return next((axes[i] + (step,) for i, step in enumerate(FACES[d]) if step))

    def beside(d):
        name, at, count, step = axis_of(d)
        return {name: at + step}

    def exists(d):
        name, at, count, step = axis_of(d)
        return at > 0 if step < 0 else at < count - 1

    loads = [
        pltpu.make_async_copy(src, dst, in_sem.at[i])
        for i, (src, dst) in enumerate([
            (pcols_hbm, pcols), (nodes_hbm, nodes), (p_hbm, p_ref),
            (scols_hbm, scols), (owners_hbm, owners), (tables_hbm, tables_ref),
        ])
    ]
    for copy in loads:
        copy.start()
    s_copies = []
    for n in range(NA):
        copy = pltpu.make_async_copy(
            s_hbm.at[pl.ds(n * SLOTS, SLOTS)], s_buf.at[pl.ds(n * SLOTS, SLOTS)], s_sem.at[n]
        )
        copy.start()
        s_copies.append(copy)

    barrier = pltpu.get_barrier_semaphore()
    others = [{"gy": lax.rem(gy + r, n_gy)} for r in range(1, n_gy)]
    greeted = jnp.int32(len(others))
    for peer in others:
        pl.semaphore_signal(barrier, inc=1, device_id=peer, device_id_type=MESH)
    for d in (0, 6, 2, 4):
        greeted = greeted + exists(d).astype(jnp.int32)

        @pl.when(exists(d))
        def _():
            pl.semaphore_signal(barrier, inc=1, device_id=beside(d), device_id_type=MESH)

    for copy in loads[:3]:
        copy.wait()

    def direction(delta):
        found = jnp.int32(SELF)
        for size in (1, whole_z, whole_y * whole_z):
            found = found + (delta >= size).astype(jnp.int32) - (delta <= -size).astype(jnp.int32)
        return found

    def own_id(n):
        return ((gx * AX + n // AY) * whole_y + gy * AY + n % AY) * whole_z + gz

    p_dir = []
    for n in range(NA):
        x, y = n // AY, n % AY
        own = own_id(n)
        p_dir.append([direction(pcols[x, y, 0, t] - own) for t in range(SLOTS)])

    row24 = lax.broadcasted_iota(jnp.int32, (24, 64), 0)
    lane192 = lax.broadcasted_iota(jnp.int32, (4, ROWS), 1)
    for n in range(NA):
        x, y = n // AY, n % AY
        live = lane192 < 3 * nodes[y, 0, x]
        for c in range(MODES):
            block = p_ref[n, c].astype(F32)
            block = jnp.where(live, block, 0.0)
            ps[0, pl.ds(n * 24 + 4 * c, 4), :] = block[:, :128]
            ps[1, pl.ds(n * 24 + 4 * c, 4), pl.ds(0, 64)] = block[:, 128:]
        code = jnp.full((24, 64), p_dir[n][0], jnp.int32)
        for t in range(1, SLOTS):
            code = jnp.where((row24 & 3) == t, p_dir[n][t], code)
        code = code * 8 + (row24 >> 2)
        ps[1, pl.ds(n * 24, 24), pl.ds(64, 64)] = code.astype(F32)
    for k in range(2):
        ps[k, pl.ds(NA * 24, 8), :] = jnp.zeros((8, 128), F32)
    for x in range(AX):
        for k in range(2):
            first, second = [ps[k, pl.ds((x * AY + y) * 24, 24), :] for y in range(AY)]
            lanes = pl.ds(k * 128, 128)
            pm[x, 0, :, lanes] = first[:16].astype(BF16)
            pm[x, 1, :, lanes] = jnp.concatenate([first[16:], second[16:]], axis=0).astype(BF16)
            pm[x, 2, :, lanes] = second[:16].astype(BF16)

    pl.semaphore_wait(barrier, greeted)

    def exchange(i, src, dst, d, send_sem, recv_sem, fill):
        copy = pltpu.make_async_remote_copy(
            src_ref=src, dst_ref=dst, send_sem=send_sem.at[i], recv_sem=recv_sem.at[i],
            device_id=beside(d), device_id_type=MESH,
        )

        @pl.when(exists(d))
        def _():
            copy.start()

        @pl.when(jnp.logical_not(exists(6 - d)))
        def _():
            fill[...] = jnp.zeros(fill.shape, fill.dtype)

        def arrived():
            @pl.when(exists(6 - d))
            def _():
                copy.wait_recv()

        def sent():
            @pl.when(exists(d))
            def _():
                copy.wait_send()

        return arrived, sent

    def halo(i, src, dst, d):
        return exchange(i, src, dst, d, ph_s, ph_r, dst)

    four = pl.ds(0, 4)
    halos = [
        halo(0, pm.at[four], pm.at[pl.ds(18, 4)], 2),
        halo(1, pm.at[four], pm.at[pl.ds(14, 4)], 4),
        halo(2, pm.at[four, pl.ds(0, 2)], pm.at[pl.ds(10, 4), pl.ds(0, 2)], 1),
        halo(3, pm.at[four, pl.ds(1, 2)], pm.at[pl.ds(6, 4), pl.ds(1, 2)], 5),
        halo(4, pm.at[0], pm.at[5], 0),
        halo(5, pm.at[3], pm.at[4], 6),
    ]
    pm[pl.ds(10, 4), 2] = jnp.zeros((4, 16, 256), BF16)
    pm[pl.ds(6, 4), 0] = jnp.zeros((4, 16, 256), BF16)

    for n in range(NA):
        halves = [
            jnp.concatenate([ps[k, pl.ds(n * 24 + t, 8, stride=4), :] for t in range(SLOTS)], axis=0)
            for k in range(2)
        ]
        own = jnp.concatenate([halves[0], halves[1][:, :64]], axis=1).astype(BF16)
        s_copies[n].wait()
        for s in range(SLOTS):
            high, low = split(dot(own, s_buf[n * SLOTS + s]))
            wb[n, pl.ds(s * 64, 32), :] = high
            wb[n, pl.ds(s * 64 + 32, 32), :] = low

    for copy in loads[3:]:
        copy.wait()
    s_dir = []
    for n in range(NA):
        x, y = n // AY, n % AY
        s_dir.append([direction(scols[x, y, 0, s] - own_id(n)) for s in range(SLOTS)])
    for arrived, _ in halos:
        arrived()

    lane128 = lax.broadcasted_iota(jnp.int32, (64, 128), 1) // 32
    terms = {d: [] for d in range(7)}

    def term(src, dst, d):
        i = sum(len(sends) for sends in terms.values())
        terms[d].append(exchange(i, src, dst, d, t_s, t_r, dst))

    for x in (0, 3, 1, 2):
        for y in range(AY):
            n = x * AY + y
            rows_of, picks = [], []
            for s in range(SLOTS):
                e = s_dir[n][s]
                at = jnp.int32(halo_place(n, 0))
                for other in range(1, 7):
                    at = jnp.where(e == other, halo_place(n, other), at)
                pair, member = at >> 1, at & 1
                own, shared = pm[pair, 2 * member], pm[pair, 1]
                rows_of += [own[:, :ROWS], shared[:, :ROWS]]
                code = jnp.concatenate([own[:, 128:], shared[:, 128:]], axis=0).astype(F32)
                code = jnp.broadcast_to(code[:, 64:65], (32, 128))
                keep = lax.broadcasted_iota(jnp.int32, (32, 128), 0) // 8
                code = jnp.where((keep < 2) | (keep == member + 2), code, -2.0)
                wanted = tables_ref[e, :, pl.ds(0, 256)]
                picks.append(
                    jnp.concatenate(
                        [
                            jnp.where(
                                code == jnp.concatenate([wanted[:, k * 128:k * 128 + 128]] * 4, axis=0), 1.0, 0.0
                            )
                            for k in range(2)
                        ],
                        axis=1,
                    ).astype(BF16)
                )
            full = dot_t(wb[n], jnp.concatenate(rows_of, axis=0))
            z = full[:64]
            for s in range(1, SLOTS):
                z = jnp.where(lane128 == s, full[s * 64:s * 64 + 64], z)
            high, low = split(z[:32] + z[32:])
            both = dot(jnp.concatenate([high, low], axis=0), jnp.concatenate(picks, axis=0))
            t_all = both[:32] + both[32:]
            for d, step in enumerate(FACES):
                block = jnp.zeros((8, 256), F32)
                for t in range(SLOTS):
                    mark = jnp.full((8, 256), p_dir[n][t], jnp.int32) == d
                    block = jnp.where(mark, t_all[t * 8:t * 8 + 8], block)
                to_x, to_y = x + step[0], y + step[1]
                if step[2]:
                    tsz[0 if step[2] < 0 else 1, x, y] = block
                elif not 0 <= to_x < AX:
                    tsx[0 if step[0] < 0 else 1, y] = block
                elif not 0 <= to_y < AY:
                    tsy[0 if step[1] < 0 else 1, x] = block
                else:
                    tbuf[d, to_x, to_y] = block
        if x == 0:
            term(tsx.at[0], tbuf.at[0, 3], 0)
        if x == 3:
            term(tsx.at[1], tbuf.at[6, 0], 6)
        term(tsz.at[0, x], tbuf.at[2, x], 2)
        term(tsz.at[1, x], tbuf.at[4, x], 4)
        term(tsy.at[0, x], tbuf.at[1, x, 1], 1)
        term(tsy.at[1, x], tbuf.at[5, x, 0], 5)

    def one_hot(source, base):
        wide = source.shape[1]
        at = lax.broadcasted_iota(jnp.int32, (128, wide), 0).astype(F32) + base
        return jnp.where(at == jnp.concatenate([source] * 16, axis=0), 1.0, 0.0).astype(BF16)

    for d in (3, 0, 6, 1, 5, 2, 4):
        for k in range(2):
            place[d, pl.ds(k * 128, 128), :] = one_hot(tables_ref[d, :, pl.ds(256, 384)], k * 128.0)
    for a in range(MODES):
        order[pl.ds(a * 128, 128), :] = one_hot(tables_ref[7], a * 128.0)

    total = jnp.zeros((128, 384), F32)
    for d in (3, 0, 6, 1, 5, 2, 4):
        for arrived, _ in terms[d]:
            arrived()
        high, low = split(tbuf[d].reshape(64, 256))
        total = total + dot(jnp.concatenate([high, low], axis=0), place[d])
    total = total[:64] + total[64:]
    for v in range(3):
        xs[v] = total[:, v * 128:v * 128 + 128]

    stacked = []
    for v in range(3):
        stacked.append(
            jnp.concatenate(
                [xs[v, pl.ds(a, 8, stride=8), :] for a in range(MODES)], axis=1
            )
        )
    high, low = split(jnp.concatenate(stacked, axis=0))
    flat = dot(jnp.concatenate([high, low], axis=0), order[...])
    flat = flat[:24] + flat[24:]
    for v in range(3):
        rows[:, pl.ds(v * PART, PART)] = flat[v * 8:v * 8 + 8, :PART]

    owner = [owners[0, gy, 0, 0, q] for q in range(NA)]
    spot = []
    for q in range(NA):
        rank = jnp.int32(0)
        for other in range(q):
            rank = rank + (owner[other] == owner[q]).astype(jnp.int32)
        spot.append(owner[q] * CAP + rank)
    row2 = lax.broadcasted_iota(jnp.int32, (CAP, WIDTH), 0)
    for target in range(n_gy):
        chosen = jnp.zeros((CAP, WIDTH), F32)
        for q in range(NA):
            row = jnp.broadcast_to(rows[pl.ds(q, 1), pl.ds(0, WIDTH)], (CAP, WIDTH))
            chosen = jnp.where(row2 + target * CAP == spot[q], row, chosen)
        sbuf[target] = chosen
    sends = []
    for r in range(1, n_gy):
        target = lax.rem(gy + r, n_gy)
        copy = pltpu.make_async_remote_copy(
            src_ref=sbuf.at[target], dst_ref=out.at[gy], send_sem=o_s.at[r - 1], recv_sem=o_r.at[r - 1],
            device_id={"gy": target}, device_id_type=MESH,
        )
        copy.start()
        sends.append(copy)
    mine = pltpu.make_async_copy(sbuf.at[gy], out.at[gy], own_sem)
    mine.start()
    for copy in sends:
        copy.wait()
    mine.wait()
    for _, sent in halos + sum(terms.values(), []):
        sent()


def local(sizes, stiff_blocks, stiff_cols, prolong_blocks, prolong_cols, agg_nodes, row_owner):
    n_gy = sizes[1]
    hbm = pl.BlockSpec(memory_space=pltpu.HBM)
    out = pl.pallas_call(
        functools.partial(kernel, sizes),
        out_shape=pltpu.VMEM((n_gy, CAP, WIDTH), F32),
        in_specs=[hbm] * 7,
        out_specs=pl.BlockSpec(memory_space=pltpu.VMEM),
        scratch_shapes=[
            pltpu.VMEM((NA, MODES, SLOTS, ROWS), BF16),
            pltpu.SMEM(stiff_cols.shape, jnp.int32),
            pltpu.SMEM(prolong_cols.shape, jnp.int32),
            pltpu.SMEM((AY, 1, AX), jnp.int32),
            pltpu.SMEM((1, n_gy, 1, 1, NA), jnp.int32),
            pltpu.VMEM((8, 8, 768), F32),
            pltpu.VMEM((NA * SLOTS, ROWS, ROWS), BF16),
            pltpu.VMEM((7, 256, 384), BF16),
            pltpu.VMEM((MODES * 128, MODES * 128), BF16),
            pltpu.VMEM((2, NA * 24 + 8, 128), F32),
            pltpu.VMEM((22, 3, 16, 256), BF16),
            pltpu.VMEM((NA, 256, ROWS), BF16),
            pltpu.VMEM((7, AX, AY, 8, 256), F32),
            pltpu.VMEM((2, AY, 8, 256), F32),
            pltpu.VMEM((2, AX, 8, 256), F32),
            pltpu.VMEM((2, AX, AY, 8, 256), F32),
            pltpu.VMEM((3, 64, 128), F32),
            pltpu.VMEM((8, 2304), F32),
            pltpu.VMEM((n_gy, CAP, WIDTH), F32),
            pltpu.SemaphoreType.DMA((6,)),
            pltpu.SemaphoreType.DMA((NA,)),
            pltpu.SemaphoreType.DMA((6,)),
            pltpu.SemaphoreType.DMA((6,)),
            pltpu.SemaphoreType.DMA((18,)),
            pltpu.SemaphoreType.DMA((18,)),
            pltpu.SemaphoreType.DMA((n_gy - 1,)),
            pltpu.SemaphoreType.DMA((n_gy - 1,)),
            pltpu.SemaphoreType.DMA,
        ],
        compiler_params=pltpu.CompilerParams(
            collective_id=0, has_side_effects=True, vmem_limit_bytes=60 * 1024 * 1024
        ),
        name="galerkin",
    )(
        prolong_blocks.transpose(0, 1, 2, 4, 3, 5).reshape(NA, MODES, SLOTS, ROWS),
        stiff_cols,
        prolong_cols,
        agg_nodes.transpose(1, 2, 0),
        row_owner.transpose(0, 1, 2, 4, 3),
        jnp.asarray(tables()),
        stiff_blocks.reshape(NA * SLOTS, ROWS, ROWS),
    )
    return out[None, :, None]


def solution(mesh):
    sizes = (mesh.shape["gx"], mesh.shape["gy"], mesh.shape["gz"])
    return jax.shard_map(
        functools.partial(local, sizes),
        mesh=mesh,
        in_specs=(
            P("gx", "gy", "gz", None, None, None),
            P("gx", "gy", "gz", None),
            P("gx", "gy", "gz", None, None, None),
            P("gx", "gy", "gz", None),
            P("gx", "gy", "gz"),
            P("gx", None, "gz", None, None),
        ),
        out_specs=P("gx", "gy", "gz", None, None),
        check_vma=False,
    )
```

```python
import functools

import jax
import jax.numpy as jnp
import numpy as np
from jax import lax
from jax.experimental import pallas as pl
from jax.experimental.pallas import tpu as pltpu
from jax.sharding import PartitionSpec as P

MESH = pl.DeviceIdType.MESH
F32 = jnp.float32
BF16 = jnp.bfloat16
AX, AY = 4, 2
NA = AX * AY
SLOTS = 4
MODES = 6
ROWS = 192
CAP = 2
WIDTH = 63 * 36
PART = 21 * 36


def points(radius):
    span = range(-radius, radius + 1)
    return [
        (x, y, z) for x in span for y in span for z in span if abs(x) + abs(y) + abs(z) <= radius
    ]


FACES, NEAR, BALL = points(1), points(2), points(3)
SELF = FACES.index((0, 0, 0))


def tables():
    table = np.full((8, 768), -1.0, np.float32)
    for e, step in enumerate(FACES):
        for d, other in enumerate(FACES):
            j = NEAR.index(tuple(p + q for p, q in zip(step, other)))
            for c in range(MODES):
                table[e, j * MODES + c] = d * 8 + c
        for j, near in enumerate(NEAR):
            o = BALL.index(tuple(p - q for p, q in zip(near, step)))
            for c in range(MODES):
                table[e, 256 + (o // 21) * 128 + (o % 21) * MODES + c] = j * MODES + c
    for a in range(MODES):
        for o in range(21):
            for c in range(MODES):
                table[7, o * 36 + a * MODES + c] = a * 128 + o * MODES + c
    return np.repeat(table[:, None], 8, axis=1)


def split(x):
    high = x.astype(BF16)
    return high, (x - high.astype(F32)).astype(BF16)


def dot(a, b):
    return jnp.dot(a, b, preferred_element_type=F32)


def dot_t(a, b):
    return lax.dot_general(a, b, (((1,), (1,)), ((), ())), preferred_element_type=F32)


def halo_place(n, e):
    x, y = n // AY, n % AY
    step = FACES[e]
    if step == (0, 0, 0):
        return n
    if step[0]:
        near = x + step[0]
        if 0 <= near < AX:
            return near * AY + y
        return (4 if step[0] < 0 else 5) * AY + y
    if step[1]:
        near = y + step[1]
        if 0 <= near < AY:
            return x * AY + near
        return (6 + x) * AY + 1 if step[1] < 0 else (10 + x) * AY
    return (14 if step[2] < 0 else 18) * AY + n


def kernel(
    sizes,
    p_hbm, scols_hbm, pcols_hbm, nodes_hbm, owners_hbm, tables_hbm, s_hbm,
    out,
    p_ref, scols, pcols, nodes, owners, tables_ref,
    s_buf, place, order, ps, pm, wb, tbuf, tsx, tsy, tsz, xs, rows, sbuf,
    in_sem, s_sem, ph_s, ph_r, t_s, t_r, o_s, o_r,
):
    n_gx, n_gy, n_gz = sizes
    gx, gy, gz = lax.axis_index("gx"), lax.axis_index("gy"), lax.axis_index("gz")
    whole_y, whole_z = AY * n_gy, n_gz
    axes = (("gx", gx, n_gx), ("gy", gy, n_gy), ("gz", gz, n_gz))

    def axis_of(d):
        return next((axes[i] + (step,) for i, step in enumerate(FACES[d]) if step))

    def beside(d):
        name, at, count, step = axis_of(d)
        return {name: at + step}

    def exists(d):
        name, at, count, step = axis_of(d)
        return at > 0 if step < 0 else at < count - 1

    loads = [
        pltpu.make_async_copy(src, dst, in_sem.at[i])
        for i, (src, dst) in enumerate([
            (pcols_hbm, pcols), (nodes_hbm, nodes), (p_hbm, p_ref),
            (scols_hbm, scols), (owners_hbm, owners), (tables_hbm, tables_ref),
        ])
    ]
    for copy in loads:
        copy.start()
    s_copies = []
    for n in range(NA):
        copy = pltpu.make_async_copy(
            s_hbm.at[pl.ds(n * SLOTS, SLOTS)], s_buf.at[pl.ds(n * SLOTS, SLOTS)], s_sem.at[n]
        )
        copy.start()
        s_copies.append(copy)

    barrier = pltpu.get_barrier_semaphore()
    others = [{"gy": lax.rem(gy + r, n_gy)} for r in range(1, n_gy)]
    greeted = jnp.int32(len(others))
    for peer in others:
        pl.semaphore_signal(barrier, inc=1, device_id=peer, device_id_type=MESH)
    for d in (0, 6, 2, 4):
        greeted = greeted + exists(d).astype(jnp.int32)

        @pl.when(exists(d))
        def _():
            pl.semaphore_signal(barrier, inc=1, device_id=beside(d), device_id_type=MESH)

    for copy in loads[:3]:
        copy.wait()

    def direction(delta):
        found = jnp.int32(SELF)
        for size in (1, whole_z, whole_y * whole_z):
            found = found + (delta >= size).astype(jnp.int32) - (delta <= -size).astype(jnp.int32)
        return found

    def own_id(n):
        return ((gx * AX + n // AY) * whole_y + gy * AY + n % AY) * whole_z + gz

    p_dir = []
    for n in range(NA):
        x, y = n // AY, n % AY
        own = own_id(n)
        p_dir.append([direction(pcols[x, y, 0, t] - own) for t in range(SLOTS)])

    row24 = lax.broadcasted_iota(jnp.int32, (24, 64), 0)
    lane192 = lax.broadcasted_iota(jnp.int32, (4, ROWS), 1)
    for n in range(NA):
        x, y = n // AY, n % AY
        live = lane192 < 3 * nodes[y, 0, x]
        for c in range(MODES):
            block = p_ref[n, c].astype(F32)
            block = jnp.where(live, block, 0.0)
            ps[0, pl.ds(n * 24 + 4 * c, 4), :] = block[:, :128]
            ps[1, pl.ds(n * 24 + 4 * c, 4), pl.ds(0, 64)] = block[:, 128:]
        code = jnp.full((24, 64), p_dir[n][0], jnp.int32)
        for t in range(1, SLOTS):
            code = jnp.where((row24 & 3) == t, p_dir[n][t], code)
        code = code * 8 + (row24 >> 2)
        ps[1, pl.ds(n * 24, 24), pl.ds(64, 64)] = code.astype(F32)
    for k in range(2):
        ps[k, pl.ds(NA * 24, 8), :] = jnp.zeros((8, 128), F32)
    for x in range(AX):
        for k in range(2):
            first, second = [ps[k, pl.ds((x * AY + y) * 24, 24), :] for y in range(AY)]
            lanes = pl.ds(k * 128, 128)
            pm[x, 0, :, lanes] = first[:16].astype(BF16)
            pm[x, 1, :, lanes] = jnp.concatenate([first[16:], second[16:]], axis=0).astype(BF16)
            pm[x, 2, :, lanes] = second[:16].astype(BF16)

    pl.semaphore_wait(barrier, greeted)

    def exchange(i, src, dst, d, send_sem, recv_sem, fill):
        copy = pltpu.make_async_remote_copy(
            src_ref=src, dst_ref=dst, send_sem=send_sem.at[i], recv_sem=recv_sem.at[i],
            device_id=beside(d), device_id_type=MESH,
        )

        @pl.when(exists(d))
        def _():
            copy.start()

        @pl.when(jnp.logical_not(exists(6 - d)))
        def _():
            fill[...] = jnp.zeros(fill.shape, fill.dtype)

        def arrived():
            @pl.when(exists(6 - d))
            def _():
                copy.wait_recv()

        def sent():
            @pl.when(exists(d))
            def _():
                copy.wait_send()

        return arrived, sent

    def halo(i, src, dst, d):
        return exchange(i, src, dst, d, ph_s, ph_r, dst)

    four = pl.ds(0, 4)
    halos = [
        halo(0, pm.at[four], pm.at[pl.ds(18, 4)], 2),
        halo(1, pm.at[four], pm.at[pl.ds(14, 4)], 4),
        halo(2, pm.at[four, pl.ds(0, 2)], pm.at[pl.ds(10, 4), pl.ds(0, 2)], 1),
        halo(3, pm.at[four, pl.ds(1, 2)], pm.at[pl.ds(6, 4), pl.ds(1, 2)], 5),
        halo(4, pm.at[0], pm.at[5], 0),
        halo(5, pm.at[3], pm.at[4], 6),
    ]
    pm[pl.ds(10, 4), 2] = jnp.zeros((4, 16, 256), BF16)
    pm[pl.ds(6, 4), 0] = jnp.zeros((4, 16, 256), BF16)

    for n in range(NA):
        halves = [
            jnp.concatenate([ps[k, pl.ds(n * 24 + t, 8, stride=4), :] for t in range(SLOTS)], axis=0)
            for k in range(2)
        ]
        own = jnp.concatenate([halves[0], halves[1][:, :64]], axis=1).astype(BF16)
        s_copies[n].wait()
        for s in range(SLOTS):
            high, low = split(dot(own, s_buf[n * SLOTS + s]))
            wb[n, pl.ds(s * 64, 32), :] = high
            wb[n, pl.ds(s * 64 + 32, 32), :] = low

    for copy in loads[3:]:
        copy.wait()
    s_dir = []
    for n in range(NA):
        x, y = n // AY, n % AY
        s_dir.append([direction(scols[x, y, 0, s] - own_id(n)) for s in range(SLOTS)])
    for arrived, _ in halos:
        arrived()

    lane128 = lax.broadcasted_iota(jnp.int32, (64, 128), 1) // 32
    terms = {d: [] for d in range(7)}

    def term(src, dst, d):
        i = sum(len(sends) for sends in terms.values())
        terms[d].append(exchange(i, src, dst, d, t_s, t_r, dst))

    for x in (0, 3, 1, 2):
        for y in range(AY):
            n = x * AY + y
            rows_of, picks = [], []
            for s in range(SLOTS):
                e = s_dir[n][s]
                at = jnp.int32(halo_place(n, 0))
                for other in range(1, 7):
                    at = jnp.where(e == other, halo_place(n, other), at)
                pair, member = at >> 1, at & 1
                own, shared = pm[pair, 2 * member], pm[pair, 1]
                rows_of += [own[:, :ROWS], shared[:, :ROWS]]
                code = jnp.concatenate([own[:, 128:], shared[:, 128:]], axis=0).astype(F32)
                code = jnp.broadcast_to(code[:, 64:65], (32, 128))
                keep = lax.broadcasted_iota(jnp.int32, (32, 128), 0) // 8
                code = jnp.where((keep < 2) | (keep == member + 2), code, -2.0)
                wanted = tables_ref[e, :, pl.ds(0, 256)]
                picks.append(
                    jnp.concatenate(
                        [
                            jnp.where(
                                code == jnp.concatenate([wanted[:, k * 128:k * 128 + 128]] * 4, axis=0), 1.0, 0.0
                            )
                            for k in range(2)
                        ],
                        axis=1,
                    ).astype(BF16)
                )
            full = dot_t(wb[n], jnp.concatenate(rows_of, axis=0))
            z = full[:64]
            for s in range(1, SLOTS):
                z = jnp.where(lane128 == s, full[s * 64:s * 64 + 64], z)
            high, low = split(z[:32] + z[32:])
            both = dot(jnp.concatenate([high, low], axis=0), jnp.concatenate(picks, axis=0))
            t_all = both[:32] + both[32:]
            for d, step in enumerate(FACES):
                block = jnp.zeros((8, 256), F32)
                for t in range(SLOTS):
                    mark = jnp.full((8, 256), p_dir[n][t], jnp.int32) == d
                    block = jnp.where(mark, t_all[t * 8:t * 8 + 8], block)
                to_x, to_y = x + step[0], y + step[1]
                if step[2]:
                    tsz[0 if step[2] < 0 else 1, x, y] = block
                elif not 0 <= to_x < AX:
                    tsx[0 if step[0] < 0 else 1, y] = block
                elif not 0 <= to_y < AY:
                    tsy[0 if step[1] < 0 else 1, x] = block
                else:
                    tbuf[d, to_x, to_y] = block
        if x == 0:
            term(tsx.at[0], tbuf.at[0, 3], 0)
        if x == 3:
            term(tsx.at[1], tbuf.at[6, 0], 6)
        term(tsz.at[0, x], tbuf.at[2, x], 2)
        term(tsz.at[1, x], tbuf.at[4, x], 4)
        term(tsy.at[0, x], tbuf.at[1, x, 1], 1)
        term(tsy.at[1, x], tbuf.at[5, x, 0], 5)

    def one_hot(source, base):
        wide = source.shape[1]
        at = lax.broadcasted_iota(jnp.int32, (128, wide), 0).astype(F32) + base
        return jnp.where(at == jnp.concatenate([source] * 16, axis=0), 1.0, 0.0).astype(BF16)

    for d in (3, 0, 6, 1, 5, 2, 4):
        for k in range(2):
            place[d, pl.ds(k * 128, 128), :] = one_hot(tables_ref[d, :, pl.ds(256, 384)], k * 128.0)
    for a in range(MODES):
        order[pl.ds(a * 128, 128), :] = one_hot(tables_ref[7], a * 128.0)

    total = jnp.zeros((128, 384), F32)
    for d in (3, 0, 6, 1, 5, 2, 4):
        for arrived, _ in terms[d]:
            arrived()
        high, low = split(tbuf[d].reshape(64, 256))
        total = total + dot(jnp.concatenate([high, low], axis=0), place[d])
    total = total[:64] + total[64:]
    for v in range(3):
        xs[v] = total[:, v * 128:v * 128 + 128]

    stacked = []
    for v in range(3):
        stacked.append(
            jnp.concatenate(
                [xs[v, pl.ds(a, 8, stride=8), :] for a in range(MODES)], axis=1
            )
        )
    high, low = split(jnp.concatenate(stacked, axis=0))
    flat = dot(jnp.concatenate([high, low], axis=0), order[...])
    flat = flat[:24] + flat[24:]
    for v in range(3):
        rows[:, pl.ds(v * PART, PART)] = flat[v * 8:v * 8 + 8, :PART]

    owner = [owners[0, gy, 0, 0, q] for q in range(NA)]
    spot = []
    for q in range(NA):
        rank = jnp.int32(0)
        for other in range(q):
            rank = rank + (owner[other] == owner[q]).astype(jnp.int32)
        spot.append(owner[q] * CAP + rank)
    row2 = lax.broadcasted_iota(jnp.int32, (CAP, WIDTH), 0)
    sends = []
    for r in sorted(range(n_gy), key=lambda r: -min(r, n_gy - r)):
        target = lax.rem(gy + r, n_gy)
        chosen = jnp.zeros((CAP, WIDTH), F32)
        for q in range(NA):
            row = jnp.broadcast_to(rows[pl.ds(q, 1), pl.ds(0, WIDTH)], (CAP, WIDTH))
            chosen = jnp.where(row2 + target * CAP == spot[q], row, chosen)
        if r == 0:
            out[gy] = chosen
            continue
        sbuf[r] = chosen
        copy = pltpu.make_async_remote_copy(
            src_ref=sbuf.at[r], dst_ref=out.at[gy], send_sem=o_s.at[r - 1], recv_sem=o_r.at[r - 1],
            device_id={"gy": target}, device_id_type=MESH,
        )
        copy.start()
        sends.append(copy)
    for copy in sends:
        copy.wait()
    for _, sent in halos + sum(terms.values(), []):
        sent()


def local(sizes, stiff_blocks, stiff_cols, prolong_blocks, prolong_cols, agg_nodes, row_owner):
    n_gy = sizes[1]
    hbm = pl.BlockSpec(memory_space=pltpu.HBM)
    out = pl.pallas_call(
        functools.partial(kernel, sizes),
        out_shape=pltpu.VMEM((n_gy, CAP, WIDTH), F32),
        in_specs=[hbm] * 7,
        out_specs=pl.BlockSpec(memory_space=pltpu.VMEM),
        scratch_shapes=[
            pltpu.VMEM((NA, MODES, SLOTS, ROWS), BF16),
            pltpu.SMEM(stiff_cols.shape, jnp.int32),
            pltpu.SMEM(prolong_cols.shape, jnp.int32),
            pltpu.SMEM((AY, 1, AX), jnp.int32),
            pltpu.SMEM((1, n_gy, 1, 1, NA), jnp.int32),
            pltpu.VMEM((8, 8, 768), F32),
            pltpu.VMEM((NA * SLOTS, ROWS, ROWS), BF16),
            pltpu.VMEM((7, 256, 384), BF16),
            pltpu.VMEM((MODES * 128, MODES * 128), BF16),
            pltpu.VMEM((2, NA * 24 + 8, 128), F32),
            pltpu.VMEM((22, 3, 16, 256), BF16),
            pltpu.VMEM((NA, 256, ROWS), BF16),
            pltpu.VMEM((7, AX, AY, 8, 256), F32),
            pltpu.VMEM((2, AY, 8, 256), F32),
            pltpu.VMEM((2, AX, 8, 256), F32),
            pltpu.VMEM((2, AX, AY, 8, 256), F32),
            pltpu.VMEM((3, 64, 128), F32),
            pltpu.VMEM((8, 2304), F32),
            pltpu.VMEM((n_gy, CAP, WIDTH), F32),
            pltpu.SemaphoreType.DMA((6,)),
            pltpu.SemaphoreType.DMA((NA,)),
            pltpu.SemaphoreType.DMA((6,)),
            pltpu.SemaphoreType.DMA((6,)),
            pltpu.SemaphoreType.DMA((18,)),
            pltpu.SemaphoreType.DMA((18,)),
            pltpu.SemaphoreType.DMA((n_gy - 1,)),
            pltpu.SemaphoreType.DMA((n_gy - 1,)),
        ],
        compiler_params=pltpu.CompilerParams(
            collective_id=0, has_side_effects=True, vmem_limit_bytes=60 * 1024 * 1024
        ),
        name="galerkin",
    )(
        prolong_blocks.transpose(0, 1, 2, 4, 3, 5).reshape(NA, MODES, SLOTS, ROWS),
        stiff_cols,
        prolong_cols,
        agg_nodes.transpose(1, 2, 0),
        row_owner.transpose(0, 1, 2, 4, 3),
        jnp.asarray(tables()),
        stiff_blocks.reshape(NA * SLOTS, ROWS, ROWS),
    )
    return out[None, :, None]


def solution(mesh):
    sizes = (mesh.shape["gx"], mesh.shape["gy"], mesh.shape["gz"])
    return jax.shard_map(
        functools.partial(local, sizes),
        mesh=mesh,
        in_specs=(
            P("gx", "gy", "gz", None, None, None),
            P("gx", "gy", "gz", None),
            P("gx", "gy", "gz", None, None, None),
            P("gx", "gy", "gz", None),
            P("gx", "gy", "gz"),
            P("gx", None, "gz", None, None),
        ),
        out_specs=P("gx", "gy", "gz", None, None),
        check_vma=False,
    )
```

```python
import functools

import jax
import jax.numpy as jnp
import numpy as np
from jax import lax
from jax.experimental import pallas as pl
from jax.experimental.pallas import tpu as pltpu
from jax.sharding import PartitionSpec as P

MESH = pl.DeviceIdType.MESH
F32 = jnp.float32
BF16 = jnp.bfloat16
AX, AY = 4, 2
NA = AX * AY
SLOTS = 4
MODES = 6
ROWS = 192
CAP = 2
WIDTH = 63 * 36
PART = 21 * 36


def points(radius):
    span = range(-radius, radius + 1)
    return [
        (x, y, z) for x in span for y in span for z in span if abs(x) + abs(y) + abs(z) <= radius
    ]


FACES, NEAR, BALL = points(1), points(2), points(3)
SELF = FACES.index((0, 0, 0))


def tables():
    table = np.full((8, 768), -1.0, np.float32)
    for e, step in enumerate(FACES):
        for d, other in enumerate(FACES):
            j = NEAR.index(tuple(p + q for p, q in zip(step, other)))
            for c in range(MODES):
                table[e, j * MODES + c] = d * 8 + c
        for j, near in enumerate(NEAR):
            o = BALL.index(tuple(p - q for p, q in zip(near, step)))
            for c in range(MODES):
                table[e, 256 + (o // 21) * 128 + (o % 21) * MODES + c] = j * MODES + c
    for a in range(MODES):
        for o in range(21):
            for c in range(MODES):
                table[7, o * 36 + a * MODES + c] = a * 128 + o * MODES + c
    return np.repeat(table[:, None], 8, axis=1)


def split(x):
    high = x.astype(BF16)
    return high, (x - high.astype(F32)).astype(BF16)


def dot(a, b):
    return jnp.dot(a, b, preferred_element_type=F32)


def dot_t(a, b):
    return lax.dot_general(a, b, (((1,), (1,)), ((), ())), preferred_element_type=F32)


def halo_place(n, e):
    x, y = n // AY, n % AY
    step = FACES[e]
    if step == (0, 0, 0):
        return n
    if step[0]:
        near = x + step[0]
        if 0 <= near < AX:
            return near * AY + y
        return (4 if step[0] < 0 else 5) * AY + y
    if step[1]:
        near = y + step[1]
        if 0 <= near < AY:
            return x * AY + near
        return (6 + x) * AY + 1 if step[1] < 0 else (10 + x) * AY
    return (14 if step[2] < 0 else 18) * AY + n


def kernel(
    sizes,
    p_hbm, scols_hbm, pcols_hbm, nodes_hbm, owners_hbm, tables_hbm, s_hbm,
    out,
    p_ref, scols, pcols, nodes, owners, tables_ref,
    s_buf, place, order, ps, pm, wb, tbuf, tsx, tsy, tsz, xs, rows, sbuf,
    in_sem, s_sem, ph_s, ph_r, t_s, t_r, o_s, o_r,
):
    n_gx, n_gy, n_gz = sizes
    gx, gy, gz = lax.axis_index("gx"), lax.axis_index("gy"), lax.axis_index("gz")
    whole_y, whole_z = AY * n_gy, n_gz
    axes = (("gx", gx, n_gx), ("gy", gy, n_gy), ("gz", gz, n_gz))

    def axis_of(d):
        return next((axes[i] + (step,) for i, step in enumerate(FACES[d]) if step))

    def beside(d):
        name, at, count, step = axis_of(d)
        return {name: at + step}

    def exists(d):
        name, at, count, step = axis_of(d)
        return at > 0 if step < 0 else at < count - 1

    loads = [
        pltpu.make_async_copy(src, dst, in_sem.at[i])
        for i, (src, dst) in enumerate([
            (pcols_hbm, pcols), (nodes_hbm, nodes), (p_hbm, p_ref),
            (scols_hbm, scols), (owners_hbm, owners), (tables_hbm, tables_ref),
        ])
    ]
    for copy in loads:
        copy.start()
    s_copies = []
    for n in range(NA):
        copy = pltpu.make_async_copy(
            s_hbm.at[pl.ds(n * SLOTS, SLOTS)], s_buf.at[pl.ds(n * SLOTS, SLOTS)], s_sem.at[n]
        )
        copy.start()
        s_copies.append(copy)

    barrier = pltpu.get_barrier_semaphore()
    others = [{"gy": lax.rem(gy + r, n_gy)} for r in range(1, n_gy)]
    greeted = jnp.int32(len(others))
    for peer in others:
        pl.semaphore_signal(barrier, inc=1, device_id=peer, device_id_type=MESH)
    for d in (0, 6, 2, 4):
        greeted = greeted + exists(d).astype(jnp.int32)

        @pl.when(exists(d))
        def _():
            pl.semaphore_signal(barrier, inc=1, device_id=beside(d), device_id_type=MESH)

    for copy in loads[:3]:
        copy.wait()

    def direction(delta):
        found = jnp.int32(SELF)
        for size in (1, whole_z, whole_y * whole_z):
            found = found + (delta >= size).astype(jnp.int32) - (delta <= -size).astype(jnp.int32)
        return found

    def own_id(n):
        return ((gx * AX + n // AY) * whole_y + gy * AY + n % AY) * whole_z + gz

    p_dir = []
    for n in range(NA):
        x, y = n // AY, n % AY
        own = own_id(n)
        p_dir.append([direction(pcols[x, y, 0, t] - own) for t in range(SLOTS)])

    row24 = lax.broadcasted_iota(jnp.int32, (24, 64), 0)
    lane192 = lax.broadcasted_iota(jnp.int32, (4, ROWS), 1)
    for n in range(NA):
        x, y = n // AY, n % AY
        live = lane192 < 3 * nodes[y, 0, x]
        for c in range(MODES):
            block = p_ref[n, c].astype(F32)
            block = jnp.where(live, block, 0.0)
            ps[0, pl.ds(n * 24 + 4 * c, 4), :] = block[:, :128]
            ps[1, pl.ds(n * 24 + 4 * c, 4), pl.ds(0, 64)] = block[:, 128:]
        code = jnp.full((24, 64), p_dir[n][0], jnp.int32)
        for t in range(1, SLOTS):
            code = jnp.where((row24 & 3) == t, p_dir[n][t], code)
        code = code * 8 + (row24 >> 2)
        ps[1, pl.ds(n * 24, 24), pl.ds(64, 64)] = code.astype(F32)
    for k in range(2):
        ps[k, pl.ds(NA * 24, 8), :] = jnp.zeros((8, 128), F32)
    for x in range(AX):
        for k in range(2):
            first, second = [ps[k, pl.ds((x * AY + y) * 24, 24), :] for y in range(AY)]
            lanes = pl.ds(k * 128, 128)
            pm[x, 0, :, lanes] = first[:16].astype(BF16)
            pm[x, 1, :, lanes] = jnp.concatenate([first[16:], second[16:]], axis=0).astype(BF16)
            pm[x, 2, :, lanes] = second[:16].astype(BF16)

    pl.semaphore_wait(barrier, greeted)

    def exchange(i, src, dst, d, send_sem, recv_sem, fill):
        copy = pltpu.make_async_remote_copy(
            src_ref=src, dst_ref=dst, send_sem=send_sem.at[i], recv_sem=recv_sem.at[i],
            device_id=beside(d), device_id_type=MESH,
        )

        @pl.when(exists(d))
        def _():
            copy.start()

        @pl.when(jnp.logical_not(exists(6 - d)))
        def _():
            fill[...] = jnp.zeros(fill.shape, fill.dtype)

        def arrived():
            @pl.when(exists(6 - d))
            def _():
                copy.wait_recv()

        def sent():
            @pl.when(exists(d))
            def _():
                copy.wait_send()

        return arrived, sent

    def halo(i, src, dst, d):
        return exchange(i, src, dst, d, ph_s, ph_r, dst)

    four = pl.ds(0, 4)
    halos = [
        halo(0, pm.at[four], pm.at[pl.ds(18, 4)], 2),
        halo(1, pm.at[four], pm.at[pl.ds(14, 4)], 4),
        halo(2, pm.at[four, pl.ds(0, 2)], pm.at[pl.ds(10, 4), pl.ds(0, 2)], 1),
        halo(3, pm.at[four, pl.ds(1, 2)], pm.at[pl.ds(6, 4), pl.ds(1, 2)], 5),
        halo(4, pm.at[0], pm.at[5], 0),
        halo(5, pm.at[3], pm.at[4], 6),
    ]
    pm[pl.ds(10, 4), 2] = jnp.zeros((4, 16, 256), BF16)
    pm[pl.ds(6, 4), 0] = jnp.zeros((4, 16, 256), BF16)

    for n in range(NA):
        halves = [
            jnp.concatenate([ps[k, pl.ds(n * 24 + t, 8, stride=4), :] for t in range(SLOTS)], axis=0)
            for k in range(2)
        ]
        own = jnp.concatenate([halves[0], halves[1][:, :64]], axis=1).astype(BF16)
        s_copies[n].wait()
        for s in range(SLOTS):
            wb[n, pl.ds(s * 32, 32), :] = dot(own, s_buf[n * SLOTS + s]).astype(BF16)

    for copy in loads[3:]:
        copy.wait()
    s_dir = []
    for n in range(NA):
        x, y = n // AY, n % AY
        s_dir.append([direction(scols[x, y, 0, s] - own_id(n)) for s in range(SLOTS)])
    for arrived, _ in halos:
        arrived()

    lane128 = lax.broadcasted_iota(jnp.int32, (32, 128), 1) // 32
    terms = {d: [] for d in range(7)}

    def term(src, dst, d):
        i = sum(len(sends) for sends in terms.values())
        terms[d].append(exchange(i, src, dst, d, t_s, t_r, dst))

    for x in (0, 3, 1, 2):
        for y in range(AY):
            n = x * AY + y
            rows_of, picks = [], []
            for s in range(SLOTS):
                e = s_dir[n][s]
                at = jnp.int32(halo_place(n, 0))
                for other in range(1, 7):
                    at = jnp.where(e == other, halo_place(n, other), at)
                pair, member = at >> 1, at & 1
                own, shared = pm[pair, 2 * member], pm[pair, 1]
                rows_of += [own[:, :ROWS], shared[:, :ROWS]]
                code = jnp.concatenate([own[:, 128:], shared[:, 128:]], axis=0).astype(F32)
                code = jnp.broadcast_to(code[:, 64:65], (32, 128))
                keep = lax.broadcasted_iota(jnp.int32, (32, 128), 0) // 8
                code = jnp.where((keep < 2) | (keep == member + 2), code, -2.0)
                wanted = tables_ref[e, :, pl.ds(0, 256)]
                picks.append(
                    jnp.concatenate(
                        [
                            jnp.where(
                                code == jnp.concatenate([wanted[:, k * 128:k * 128 + 128]] * 4, axis=0), 1.0, 0.0
                            )
                            for k in range(2)
                        ],
                        axis=1,
                    ).astype(BF16)
                )
            full = dot_t(wb[n], jnp.concatenate(rows_of, axis=0))
            z = full[:32]
            for s in range(1, SLOTS):
                z = jnp.where(lane128 == s, full[s * 32:s * 32 + 32], z)
            high, low = split(z)
            both = dot(jnp.concatenate([high, low], axis=0), jnp.concatenate(picks, axis=0))
            t_all = both[:32] + both[32:]
            for d, step in enumerate(FACES):
                block = jnp.zeros((8, 256), F32)
                for t in range(SLOTS):
                    mark = jnp.full((8, 256), p_dir[n][t], jnp.int32) == d
                    block = jnp.where(mark, t_all[t * 8:t * 8 + 8], block)
                to_x, to_y = x + step[0], y + step[1]
                if step[2]:
                    tsz[0 if step[2] < 0 else 1, x, y] = block
                elif not 0 <= to_x < AX:
                    tsx[0 if step[0] < 0 else 1, y] = block
                elif not 0 <= to_y < AY:
                    tsy[0 if step[1] < 0 else 1, x] = block
                else:
                    tbuf[d, to_x, to_y] = block
        if x == 0:
            term(tsx.at[0], tbuf.at[0, 3], 0)
        if x == 3:
            term(tsx.at[1], tbuf.at[6, 0], 6)
        term(tsz.at[0, x], tbuf.at[2, x], 2)
        term(tsz.at[1, x], tbuf.at[4, x], 4)
        term(tsy.at[0, x], tbuf.at[1, x, 1], 1)
        term(tsy.at[1, x], tbuf.at[5, x, 0], 5)

    def one_hot(source, base):
        wide = source.shape[1]
        at = lax.broadcasted_iota(jnp.int32, (128, wide), 0).astype(F32) + base
        return jnp.where(at == jnp.concatenate([source] * 16, axis=0), 1.0, 0.0).astype(BF16)

    for d in (3, 0, 6, 1, 5, 2, 4):
        for k in range(2):
            place[d, pl.ds(k * 128, 128), :] = one_hot(tables_ref[d, :, pl.ds(256, 384)], k * 128.0)
    for a in range(MODES):
        order[pl.ds(a * 128, 128), :] = one_hot(tables_ref[7], a * 128.0)

    total = jnp.zeros((128, 384), F32)
    for d in (3, 0, 6, 1, 5, 2, 4):
        for arrived, _ in terms[d]:
            arrived()
        high, low = split(tbuf[d].reshape(64, 256))
        total = total + dot(jnp.concatenate([high, low], axis=0), place[d])
    total = total[:64] + total[64:]
    for v in range(3):
        xs[v] = total[:, v * 128:v * 128 + 128]

    stacked = []
    for v in range(3):
        stacked.append(
            jnp.concatenate(
                [xs[v, pl.ds(a, 8, stride=8), :] for a in range(MODES)], axis=1
            )
        )
    high, low = split(jnp.concatenate(stacked, axis=0))
    flat = dot(jnp.concatenate([high, low], axis=0), order[...])
    flat = flat[:24] + flat[24:]
    for v in range(3):
        rows[:, pl.ds(v * PART, PART)] = flat[v * 8:v * 8 + 8, :PART]

    owner = [owners[0, gy, 0, 0, q] for q in range(NA)]
    spot = []
    for q in range(NA):
        rank = jnp.int32(0)
        for other in range(q):
            rank = rank + (owner[other] == owner[q]).astype(jnp.int32)
        spot.append(owner[q] * CAP + rank)
    row2 = lax.broadcasted_iota(jnp.int32, (CAP, WIDTH), 0)
    sends = []
    for r in sorted(range(n_gy), key=lambda r: -min(r, n_gy - r)):
        target = lax.rem(gy + r, n_gy)
        chosen = jnp.zeros((CAP, WIDTH), F32)
        for q in range(NA):
            row = jnp.broadcast_to(rows[pl.ds(q, 1), pl.ds(0, WIDTH)], (CAP, WIDTH))
            chosen = jnp.where(row2 + target * CAP == spot[q], row, chosen)
        if r == 0:
            out[gy] = chosen
            continue
        sbuf[r] = chosen
        copy = pltpu.make_async_remote_copy(
            src_ref=sbuf.at[r], dst_ref=out.at[gy], send_sem=o_s.at[r - 1], recv_sem=o_r.at[r - 1],
            device_id={"gy": target}, device_id_type=MESH,
        )
        copy.start()
        sends.append(copy)
    for copy in sends:
        copy.wait()
    for _, sent in halos + sum(terms.values(), []):
        sent()


def local(sizes, stiff_blocks, stiff_cols, prolong_blocks, prolong_cols, agg_nodes, row_owner):
    n_gy = sizes[1]
    hbm = pl.BlockSpec(memory_space=pltpu.HBM)
    out = pl.pallas_call(
        functools.partial(kernel, sizes),
        out_shape=pltpu.VMEM((n_gy, CAP, WIDTH), F32),
        in_specs=[hbm] * 7,
        out_specs=pl.BlockSpec(memory_space=pltpu.VMEM),
        scratch_shapes=[
            pltpu.VMEM((NA, MODES, SLOTS, ROWS), BF16),
            pltpu.SMEM(stiff_cols.shape, jnp.int32),
            pltpu.SMEM(prolong_cols.shape, jnp.int32),
            pltpu.SMEM((AY, 1, AX), jnp.int32),
            pltpu.SMEM((1, n_gy, 1, 1, NA), jnp.int32),
            pltpu.VMEM((8, 8, 768), F32),
            pltpu.VMEM((NA * SLOTS, ROWS, ROWS), BF16),
            pltpu.VMEM((7, 256, 384), BF16),
            pltpu.VMEM((MODES * 128, MODES * 128), BF16),
            pltpu.VMEM((2, NA * 24 + 8, 128), F32),
            pltpu.VMEM((22, 3, 16, 256), BF16),
            pltpu.VMEM((NA, 128, ROWS), BF16),
            pltpu.VMEM((7, AX, AY, 8, 256), F32),
            pltpu.VMEM((2, AY, 8, 256), F32),
            pltpu.VMEM((2, AX, 8, 256), F32),
            pltpu.VMEM((2, AX, AY, 8, 256), F32),
            pltpu.VMEM((3, 64, 128), F32),
            pltpu.VMEM((8, 2304), F32),
            pltpu.VMEM((n_gy, CAP, WIDTH), F32),
            pltpu.SemaphoreType.DMA((6,)),
            pltpu.SemaphoreType.DMA((NA,)),
            pltpu.SemaphoreType.DMA((6,)),
            pltpu.SemaphoreType.DMA((6,)),
            pltpu.SemaphoreType.DMA((18,)),
            pltpu.SemaphoreType.DMA((18,)),
            pltpu.SemaphoreType.DMA((n_gy - 1,)),
            pltpu.SemaphoreType.DMA((n_gy - 1,)),
        ],
        compiler_params=pltpu.CompilerParams(
            collective_id=0, has_side_effects=True, vmem_limit_bytes=60 * 1024 * 1024
        ),
        name="galerkin",
    )(
        prolong_blocks.transpose(0, 1, 2, 4, 3, 5).reshape(NA, MODES, SLOTS, ROWS),
        stiff_cols,
        prolong_cols,
        agg_nodes.transpose(1, 2, 0),
        row_owner.transpose(0, 1, 2, 4, 3),
        jnp.asarray(tables()),
        stiff_blocks.reshape(NA * SLOTS, ROWS, ROWS),
    )
    return out[None, :, None]


def solution(mesh):
    sizes = (mesh.shape["gx"], mesh.shape["gy"], mesh.shape["gz"])
    return jax.shard_map(
        functools.partial(local, sizes),
        mesh=mesh,
        in_specs=(
            P("gx", "gy", "gz", None, None, None),
            P("gx", "gy", "gz", None),
            P("gx", "gy", "gz", None, None, None),
            P("gx", "gy", "gz", None),
            P("gx", "gy", "gz"),
            P("gx", None, "gz", None, None),
        ),
        out_specs=P("gx", "gy", "gz", None, None),
        check_vma=False,
    )
```

```python
import functools

import jax
import jax.numpy as jnp
import numpy as np
from jax import lax
from jax.experimental import pallas as pl
from jax.experimental.pallas import tpu as pltpu
from jax.sharding import PartitionSpec as P

MESH = pl.DeviceIdType.MESH
F32 = jnp.float32
BF16 = jnp.bfloat16
AX, AY = 4, 2
NA = AX * AY
SLOTS = 4
MODES = 6
ROWS = 192
CAP = 2
WIDTH = 63 * 36
PART = 21 * 36


def points(radius):
    span = range(-radius, radius + 1)
    return [
        (x, y, z) for x in span for y in span for z in span if abs(x) + abs(y) + abs(z) <= radius
    ]


FACES, NEAR, BALL = points(1), points(2), points(3)
SELF = FACES.index((0, 0, 0))


def tables():
    table = np.full((8, 768), -1.0, np.float32)
    for e, step in enumerate(FACES):
        for d, other in enumerate(FACES):
            j = NEAR.index(tuple(p + q for p, q in zip(step, other)))
            for c in range(MODES):
                table[e, j * MODES + c] = d * 8 + c
        for j, near in enumerate(NEAR):
            o = BALL.index(tuple(p - q for p, q in zip(near, step)))
            for c in range(MODES):
                table[e, 256 + (o // 21) * 128 + (o % 21) * MODES + c] = j * MODES + c
    for a in range(MODES):
        for o in range(21):
            for c in range(MODES):
                table[7, o * 36 + a * MODES + c] = a * 128 + o * MODES + c
    return np.repeat(table[:, None], 8, axis=1)


def split(x):
    high = x.astype(BF16)
    return high, (x - high.astype(F32)).astype(BF16)


def dot(a, b):
    return jnp.dot(a, b, preferred_element_type=F32)


def dot_t(a, b):
    return lax.dot_general(a, b, (((1,), (1,)), ((), ())), preferred_element_type=F32)


def halo_place(n, e):
    x, y = n // AY, n % AY
    step = FACES[e]
    if step == (0, 0, 0):
        return n
    if step[0]:
        near = x + step[0]
        if 0 <= near < AX:
            return near * AY + y
        return (4 if step[0] < 0 else 5) * AY + y
    if step[1]:
        near = y + step[1]
        if 0 <= near < AY:
            return x * AY + near
        return (6 + x) * AY + 1 if step[1] < 0 else (10 + x) * AY
    return (14 if step[2] < 0 else 18) * AY + n


def kernel(
    sizes,
    p_hbm, scols_hbm, pcols_hbm, nodes_hbm, owners_hbm, tables_hbm, s_hbm,
    out,
    p_ref, scols, pcols, nodes, owners, tables_ref,
    s_buf, place, order, ps, pm, wb, tbuf, tsx, tsy, tsz, xs, rows, sbuf,
    in_sem, s_sem, ph_s, ph_r, t_s, t_r, o_s, o_r,
):
    n_gx, n_gy, n_gz = sizes
    gx, gy, gz = lax.axis_index("gx"), lax.axis_index("gy"), lax.axis_index("gz")
    whole_y, whole_z = AY * n_gy, n_gz
    axes = (("gx", gx, n_gx), ("gy", gy, n_gy), ("gz", gz, n_gz))

    def axis_of(d):
        return next((axes[i] + (step,) for i, step in enumerate(FACES[d]) if step))

    def beside(d):
        name, at, count, step = axis_of(d)
        return {name: at + step}

    def exists(d):
        name, at, count, step = axis_of(d)
        return at > 0 if step < 0 else at < count - 1

    loads = [
        pltpu.make_async_copy(src, dst, in_sem.at[i])
        for i, (src, dst) in enumerate([
            (pcols_hbm, pcols), (nodes_hbm, nodes), (p_hbm, p_ref),
            (scols_hbm, scols), (owners_hbm, owners), (tables_hbm, tables_ref),
        ])
    ]
    for copy in loads:
        copy.start()
    s_copies = []
    for n in range(NA):
        copy = pltpu.make_async_copy(
            s_hbm.at[pl.ds(n * SLOTS, SLOTS)], s_buf.at[pl.ds(n * SLOTS, SLOTS)], s_sem.at[n]
        )
        copy.start()
        s_copies.append(copy)

    barrier = pltpu.get_barrier_semaphore()
    others = [{"gy": lax.rem(gy + r, n_gy)} for r in range(1, n_gy)]
    greeted = jnp.int32(len(others))
    for peer in others:
        pl.semaphore_signal(barrier, inc=1, device_id=peer, device_id_type=MESH)
    for d in (0, 6, 2, 4):
        greeted = greeted + exists(d).astype(jnp.int32)

        @pl.when(exists(d))
        def _():
            pl.semaphore_signal(barrier, inc=1, device_id=beside(d), device_id_type=MESH)

    for copy in loads[:3]:
        copy.wait()

    def direction(delta):
        found = jnp.int32(SELF)
        for size in (1, whole_z, whole_y * whole_z):
            found = found + (delta >= size).astype(jnp.int32) - (delta <= -size).astype(jnp.int32)
        return found

    def own_id(n):
        return ((gx * AX + n // AY) * whole_y + gy * AY + n % AY) * whole_z + gz

    p_dir = []
    for n in range(NA):
        x, y = n // AY, n % AY
        own = own_id(n)
        p_dir.append([direction(pcols[x, y, 0, t] - own) for t in range(SLOTS)])

    row24 = lax.broadcasted_iota(jnp.int32, (24, 64), 0)
    lane192 = lax.broadcasted_iota(jnp.int32, (4, ROWS), 1)
    for n in range(NA):
        x, y = n // AY, n % AY
        live = lane192 < 3 * nodes[y, 0, x]
        for c in range(MODES):
            block = p_ref[n, c].astype(F32)
            block = jnp.where(live, block, 0.0)
            ps[0, pl.ds(n * 24 + 4 * c, 4), :] = block[:, :128]
            ps[1, pl.ds(n * 24 + 4 * c, 4), pl.ds(0, 64)] = block[:, 128:]
        code = jnp.full((24, 64), p_dir[n][0], jnp.int32)
        for t in range(1, SLOTS):
            code = jnp.where((row24 & 3) == t, p_dir[n][t], code)
        code = code * 8 + (row24 >> 2)
        ps[1, pl.ds(n * 24, 24), pl.ds(64, 64)] = code.astype(F32)
    for k in range(2):
        ps[k, pl.ds(NA * 24, 8), :] = jnp.zeros((8, 128), F32)
    for x in range(AX):
        for k in range(2):
            first, second = [ps[k, pl.ds((x * AY + y) * 24, 24), :] for y in range(AY)]
            lanes = pl.ds(k * 128, 128)
            pm[x, 0, :, lanes] = first[:16].astype(BF16)
            pm[x, 1, :, lanes] = jnp.concatenate([first[16:], second[16:]], axis=0).astype(BF16)
            pm[x, 2, :, lanes] = second[:16].astype(BF16)

    pl.semaphore_wait(barrier, greeted)

    def exchange(i, src, dst, d, send_sem, recv_sem, fill):
        copy = pltpu.make_async_remote_copy(
            src_ref=src, dst_ref=dst, send_sem=send_sem.at[i], recv_sem=recv_sem.at[i],
            device_id=beside(d), device_id_type=MESH,
        )

        @pl.when(exists(d))
        def _():
            copy.start()

        @pl.when(jnp.logical_not(exists(6 - d)))
        def _():
            fill[...] = jnp.zeros(fill.shape, fill.dtype)

        def arrived():
            @pl.when(exists(6 - d))
            def _():
                copy.wait_recv()

        def sent():
            @pl.when(exists(d))
            def _():
                copy.wait_send()

        return arrived, sent

    def halo(i, src, dst, d):
        return exchange(i, src, dst, d, ph_s, ph_r, dst)

    four = pl.ds(0, 4)
    halos = [
        halo(0, pm.at[four], pm.at[pl.ds(18, 4)], 2),
        halo(1, pm.at[four], pm.at[pl.ds(14, 4)], 4),
        halo(2, pm.at[four, pl.ds(0, 2)], pm.at[pl.ds(10, 4), pl.ds(0, 2)], 1),
        halo(3, pm.at[four, pl.ds(1, 2)], pm.at[pl.ds(6, 4), pl.ds(1, 2)], 5),
        halo(4, pm.at[0], pm.at[5], 0),
        halo(5, pm.at[3], pm.at[4], 6),
    ]
    pm[pl.ds(10, 4), 2] = jnp.zeros((4, 16, 256), BF16)
    pm[pl.ds(6, 4), 0] = jnp.zeros((4, 16, 256), BF16)

    for n in range(NA):
        halves = [
            jnp.concatenate([ps[k, pl.ds(n * 24 + t, 8, stride=4), :] for t in range(SLOTS)], axis=0)
            for k in range(2)
        ]
        own = jnp.concatenate([halves[0], halves[1][:, :64]], axis=1).astype(BF16)
        s_copies[n].wait()
        for s in range(SLOTS):
            wb[n, pl.ds(s * 32, 32), :] = dot(own, s_buf[n * SLOTS + s]).astype(BF16)

    for copy in loads[3:]:
        copy.wait()
    s_dir = []
    for n in range(NA):
        x, y = n // AY, n % AY
        s_dir.append([direction(scols[x, y, 0, s] - own_id(n)) for s in range(SLOTS)])
    for arrived, _ in halos:
        arrived()

    lane128 = lax.broadcasted_iota(jnp.int32, (32, 128), 1) // 32
    terms = {d: [] for d in range(7)}

    def term(src, dst, d):
        i = sum(len(sends) for sends in terms.values())
        terms[d].append(exchange(i, src, dst, d, t_s, t_r, dst))

    for first, second in ((0, 3), (1, 2)):
        for x, y in ((first, 0), (first, 1), (second, 0), (second, 1)):
            n = x * AY + y
            rows_of, picks = [], []
            for s in range(SLOTS):
                e = s_dir[n][s]
                at = jnp.int32(halo_place(n, 0))
                for other in range(1, 7):
                    at = jnp.where(e == other, halo_place(n, other), at)
                pair, member = at >> 1, at & 1
                own, shared = pm[pair, 2 * member], pm[pair, 1]
                rows_of += [own[:, :ROWS], shared[:, :ROWS]]
                code = jnp.concatenate([own[:, 128:], shared[:, 128:]], axis=0).astype(F32)
                code = jnp.broadcast_to(code[:, 64:65], (32, 128))
                keep = lax.broadcasted_iota(jnp.int32, (32, 128), 0) // 8
                code = jnp.where((keep < 2) | (keep == member + 2), code, -2.0)
                wanted = tables_ref[e, :, pl.ds(0, 256)]
                picks.append(
                    jnp.concatenate(
                        [
                            jnp.where(
                                code == jnp.concatenate([wanted[:, k * 128:k * 128 + 128]] * 4, axis=0), 1.0, 0.0
                            )
                            for k in range(2)
                        ],
                        axis=1,
                    ).astype(BF16)
                )
            full = dot_t(wb[n], jnp.concatenate(rows_of, axis=0))
            z = full[:32]
            for s in range(1, SLOTS):
                z = jnp.where(lane128 == s, full[s * 32:s * 32 + 32], z)
            high, low = split(z)
            both = dot(jnp.concatenate([high, low], axis=0), jnp.concatenate(picks, axis=0))
            t_all = both[:32] + both[32:]
            for d, step in enumerate(FACES):
                block = jnp.zeros((8, 256), F32)
                for t in range(SLOTS):
                    mark = jnp.full((8, 256), p_dir[n][t], jnp.int32) == d
                    block = jnp.where(mark, t_all[t * 8:t * 8 + 8], block)
                to_x, to_y = x + step[0], y + step[1]
                if step[2]:
                    tsz[0 if step[2] < 0 else 1, x, y] = block
                elif not 0 <= to_x < AX:
                    tsx[0 if step[0] < 0 else 1, y] = block
                elif not 0 <= to_y < AY:
                    tsy[0 if step[1] < 0 else 1, x] = block
                else:
                    tbuf[d, to_x, to_y] = block
        for x in (first, second):
            if x == 0:
                term(tsx.at[0], tbuf.at[0, 3], 0)
            if x == 3:
                term(tsx.at[1], tbuf.at[6, 0], 6)
            term(tsz.at[0, x], tbuf.at[2, x], 2)
            term(tsz.at[1, x], tbuf.at[4, x], 4)
            term(tsy.at[0, x], tbuf.at[1, x, 1], 1)
            term(tsy.at[1, x], tbuf.at[5, x, 0], 5)

    def one_hot(source, base):
        wide = source.shape[1]
        at = lax.broadcasted_iota(jnp.int32, (128, wide), 0).astype(F32) + base
        return jnp.where(at == jnp.concatenate([source] * 16, axis=0), 1.0, 0.0).astype(BF16)

    for d in (3, 0, 6, 1, 5, 2, 4):
        for k in range(2):
            place[d, pl.ds(k * 128, 128), :] = one_hot(tables_ref[d, :, pl.ds(256, 384)], k * 128.0)
    for a in range(MODES):
        order[pl.ds(a * 128, 128), :] = one_hot(tables_ref[7], a * 128.0)

    total = jnp.zeros((128, 384), F32)
    for d in (3, 0, 6, 1, 5, 2, 4):
        for arrived, _ in terms[d]:
            arrived()
        high, low = split(tbuf[d].reshape(64, 256))
        total = total + dot(jnp.concatenate([high, low], axis=0), place[d])
    total = total[:64] + total[64:]
    for v in range(3):
        xs[v] = total[:, v * 128:v * 128 + 128]

    stacked = []
    for v in range(3):
        stacked.append(
            jnp.concatenate(
                [xs[v, pl.ds(a, 8, stride=8), :] for a in range(MODES)], axis=1
            )
        )
    high, low = split(jnp.concatenate(stacked, axis=0))
    flat = dot(jnp.concatenate([high, low], axis=0), order[...])
    flat = flat[:24] + flat[24:]
    for v in range(3):
        rows[:, pl.ds(v * PART, PART)] = flat[v * 8:v * 8 + 8, :PART]

    owner = [owners[0, gy, 0, 0, q] for q in range(NA)]
    spot = []
    for q in range(NA):
        rank = jnp.int32(0)
        for other in range(q):
            rank = rank + (owner[other] == owner[q]).astype(jnp.int32)
        spot.append(owner[q] * CAP + rank)
    row2 = lax.broadcasted_iota(jnp.int32, (CAP, WIDTH), 0)
    sends = []
    for r in sorted(range(n_gy), key=lambda r: -min(r, n_gy - r)):
        target = lax.rem(gy + r, n_gy)
        chosen = jnp.zeros((CAP, WIDTH), F32)
        for q in range(NA):
            row = jnp.broadcast_to(rows[pl.ds(q, 1), pl.ds(0, WIDTH)], (CAP, WIDTH))
            chosen = jnp.where(row2 + target * CAP == spot[q], row, chosen)
        if r == 0:
            out[gy] = chosen
            continue
        sbuf[r] = chosen
        copy = pltpu.make_async_remote_copy(
            src_ref=sbuf.at[r], dst_ref=out.at[gy], send_sem=o_s.at[r - 1], recv_sem=o_r.at[r - 1],
            device_id={"gy": target}, device_id_type=MESH,
        )
        copy.start()
        sends.append(copy)
    for copy in sends:
        copy.wait()
    for _, sent in halos + sum(terms.values(), []):
        sent()


def local(sizes, stiff_blocks, stiff_cols, prolong_blocks, prolong_cols, agg_nodes, row_owner):
    n_gy = sizes[1]
    hbm = pl.BlockSpec(memory_space=pltpu.HBM)
    out = pl.pallas_call(
        functools.partial(kernel, sizes),
        out_shape=pltpu.VMEM((n_gy, CAP, WIDTH), F32),
        in_specs=[hbm] * 7,
        out_specs=pl.BlockSpec(memory_space=pltpu.VMEM),
        scratch_shapes=[
            pltpu.VMEM((NA, MODES, SLOTS, ROWS), BF16),
            pltpu.SMEM(stiff_cols.shape, jnp.int32),
            pltpu.SMEM(prolong_cols.shape, jnp.int32),
            pltpu.SMEM((AY, 1, AX), jnp.int32),
            pltpu.SMEM((1, n_gy, 1, 1, NA), jnp.int32),
            pltpu.VMEM((8, 8, 768), F32),
            pltpu.VMEM((NA * SLOTS, ROWS, ROWS), BF16),
            pltpu.VMEM((7, 256, 384), BF16),
            pltpu.VMEM((MODES * 128, MODES * 128), BF16),
            pltpu.VMEM((2, NA * 24 + 8, 128), F32),
            pltpu.VMEM((22, 3, 16, 256), BF16),
            pltpu.VMEM((NA, 128, ROWS), BF16),
            pltpu.VMEM((7, AX, AY, 8, 256), F32),
            pltpu.VMEM((2, AY, 8, 256), F32),
            pltpu.VMEM((2, AX, 8, 256), F32),
            pltpu.VMEM((2, AX, AY, 8, 256), F32),
            pltpu.VMEM((3, 64, 128), F32),
            pltpu.VMEM((8, 2304), F32),
            pltpu.VMEM((n_gy, CAP, WIDTH), F32),
            pltpu.SemaphoreType.DMA((6,)),
            pltpu.SemaphoreType.DMA((NA,)),
            pltpu.SemaphoreType.DMA((6,)),
            pltpu.SemaphoreType.DMA((6,)),
            pltpu.SemaphoreType.DMA((18,)),
            pltpu.SemaphoreType.DMA((18,)),
            pltpu.SemaphoreType.DMA((n_gy - 1,)),
            pltpu.SemaphoreType.DMA((n_gy - 1,)),
        ],
        compiler_params=pltpu.CompilerParams(
            collective_id=0, has_side_effects=True, vmem_limit_bytes=60 * 1024 * 1024
        ),
        name="galerkin",
    )(
        prolong_blocks.transpose(0, 1, 2, 4, 3, 5).reshape(NA, MODES, SLOTS, ROWS),
        stiff_cols,
        prolong_cols,
        agg_nodes.transpose(1, 2, 0),
        row_owner.transpose(0, 1, 2, 4, 3),
        jnp.asarray(tables()),
        stiff_blocks.reshape(NA * SLOTS, ROWS, ROWS),
    )
    return out[None, :, None]


def solution(mesh):
    sizes = (mesh.shape["gx"], mesh.shape["gy"], mesh.shape["gz"])
    return jax.shard_map(
        functools.partial(local, sizes),
        mesh=mesh,
        in_specs=(
            P("gx", "gy", "gz", None, None, None),
            P("gx", "gy", "gz", None),
            P("gx", "gy", "gz", None, None, None),
            P("gx", "gy", "gz", None),
            P("gx", "gy", "gz"),
            P("gx", None, "gz", None, None),
        ),
        out_specs=P("gx", "gy", "gz", None, None),
        check_vma=False,
    )
```
